32 devices in a mesh: center: 8 (over y, x, core), expert: 4 (over z).
Axes of the slice: x: 2, y: 2, z: 4, core: 2. Of those that a mesh axis runs over, the one named last changes fastest.
Arguments:
- tokens: bfloat16 [4096, 2048], P(('center', 'expert')), may hold values from -6 to 6
- doc_ids: int32 [32, 128], P(('center', 'expert')), may hold values from 0 to 7, never falling along the last dimension, each value on 1 to 32 neighbouring positions
- expert_ids: int32 [4096, 8], P(('center', 'expert')), may hold values from 0 to 31, all different within a row; in each aligned block of 128 rows (0 to 127, 128 to 255, ...) at most 64 rows name the same one
- gate_raw: float32 [4096, 8], P(('center', 'expert')), may hold values from 0.1 to 1
- gate_up: bfloat16 [32, 2048, 1536], P(('center', 'expert')), may hold values from -0.125 to 0.125
- down: bfloat16 [32, 768, 2048], P(('center', 'expert'))
- bank: bfloat16 [16384, 2048], P('center')
Outputs:
- layer_out: bfloat16 [4096, 2048], P(('center', 'expert'))
- scores: float32 [256], P(('center', 'expert'))
The draws below stay inside these ranges and needn't reach their ends.
Inputs may be any that keep to these rules, and one draw needn't show every extreme that they name: `expert_ids`: each row names 8 different experts; in the rows of one device no expert is named by more than 64 rows, a bound that some block reaches. `doc_ids`: each row splits its 128 tokens into 8 runs numbered in order, each of 1 to 32 tokens, one of exactly 32.
All inputs are finite; a program needn't handle non-finite values.
Results may differ from the reference program's by a relative error of at most 0.0071.
Values may be sent and summed in bfloat16 or wider, within the bound.
No kernel may reach another device: no remote copies, remote signals or barrier semaphores. Data moves between devices by JAX's collectives and lax.ppermute only.
A program may use at most 128 MiB of HBM per device.

```python
import math
import jax
import jax.numpy as jnp
import numpy as np
from jax import lax

D = 2048
FF = 768
TOP = 8
TOK_DEV = 128
DOC_MOST = 32
SHARDS = 32
EXPERTS = 32
CAP = 64
DOC_DEV = 8
TOKENS = 4096
DOCS = 256
CENTERS = 16384


def shared_features(key):
    chosen_count = min(16, D // 4)
    feature_order = jax.random.permutation(jax.random.fold_in(key, 9173), D)
    strong = (feature_order < chosen_count).astype(jnp.float32)
    return (strong, chosen_count)


def draw_down(key, part):
    strong, chosen_count = shared_features(key)
    own_key = jax.random.fold_in(key, 311)
    values = jnp.clip(jax.random.normal(own_key, (EXPERTS, FF, D), jnp.float32), -4.0, 4.0)
    column_scale = (0.5 + 5.5 * strong) / math.sqrt(FF)
    return (values * column_scale[None, None, :]).astype(jnp.bfloat16)


def draw_bank(key, part):
    strong, chosen_count = shared_features(key)
    direction_key = jax.random.fold_in(key, 401)
    rough_key = jax.random.fold_in(key, 402)
    radius_key = jax.random.fold_in(key, 403)
    direction = jnp.clip(jax.random.normal(direction_key, (CENTERS, D), jnp.float32), -4.0, 4.0)
    rough = jnp.clip(jax.random.normal(rough_key, (CENTERS, D), jnp.float32), -4.0, 4.0)
    radius = jnp.exp(jax.random.uniform(radius_key, (CENTERS,), jnp.float32, math.log(0.35), math.log(1.0)))
    planted = radius[:, None] * direction * strong[None, :] / math.sqrt(chosen_count)
    background = 0.3 * rough * (1.0 - strong[None, :]) / math.sqrt(D)
    return (planted + background).astype(jnp.bfloat16)


def level_of(stream_key, dims, pieces, least, high):
    gain = 1.0
    for axis_at, parts in pieces:
        heights = jax.random.uniform(jax.random.fold_in(jax.random.fold_in(stream_key, 6), axis_at), (parts,), jnp.float32, least / len(pieces), high / len(pieces))
        gain = gain * jnp.repeat(jnp.exp(heights), dims[axis_at] // parts).reshape((-1,) + (1,) * (len(dims) - 1 - axis_at))
    return gain


def profile(amount, total, most, slope):
    portions = [(1 << 20) // math.isqrt(standing ** slope) + 1 for standing in range(2, amount + 1)]
    surplus, counts = total - most - (amount - 1), [1] * (amount - 1)
    while surplus > 0:
        candidates = [i for i in range(amount - 1) if counts[i] < most]
        pool, remaining = sum([portions[i] for i in candidates]), surplus
        for i in candidates:
            extra = min(most - counts[i], max(1, remaining * portions[i] // pool), surplus)
            counts[i] = counts[i] + extra
            surplus = surplus - extra
    return np.array([most] + counts)


def ragged(key, number_of, total, bound, slope):
    if number_of == 2:
        one = jax.random.randint(key, (), max(1, total - bound), min(bound, total - 1) + 1)
        return jnp.stack([one, total - one])
    lengths = jnp.asarray(profile(number_of, total, bound, slope), jnp.int32)
    pairs = (number_of - 1) // 2
    donor, taker = lengths[1:1 + 2 * pairs:2], lengths[2:2 + 2 * pairs:2]
    room = jnp.minimum(donor - 1, bound - taker)
    moved = jax.random.randint(jax.random.fold_in(key, 1), (pairs,), 0, 1 << 20) % (room + 1)
    lengths = lengths.at[1:1 + 2 * pairs:2].set(donor - moved).at[2:2 + 2 * pairs:2].set(taker + moved)
    return lengths[jax.random.permutation(jax.random.fold_in(key, 2), number_of)]


def assign_block(key, own, number, rows, amount, top, most, lean):
    sequence = jax.random.permutation(key, amount)
    crowded, common = load_shares(amount, rows * top, most, lean, True), load_shares(amount, rows * top, most, lean, False)
    places = jnp.arange(amount)

    def named(lengths, rotation):
        used = int((lengths > 0).sum())
        fixed = max(1, used // 4)
        moved = fixed + (places - fixed + rotation * (used - fixed)) % max(1, amount - fixed)
        return jnp.zeros((amount,), jnp.int32).at[sequence[jnp.where(places < fixed, places, moved)]].set(jnp.asarray(lengths, jnp.int32))

    lengths = jnp.where(number % 4 == 0, named(crowded, number // 4), named(common, number - number // 4 - 1))
    mixed = jax.random.permutation(jax.random.fold_in(own, 3), amount)
    source_of, sink = mixed[0:amount // 2 * 2:2], mixed[1:amount // 2 * 2:2]
    room = jnp.minimum(lengths[source_of] - 1, most - lengths[sink]) // 2
    room = jnp.where((source_of == sequence[0]) | (sink == sequence[0]) | (lengths[sink] == 0), 0, jnp.maximum(room, 0))
    moved = jax.random.randint(jax.random.fold_in(own, 4), (amount // 2,), 0, 1 << 20) % (room + 1)
    lengths = lengths.at[source_of].add(-moved).at[sink].add(moved)
    members = jnp.searchsorted(jnp.cumsum(lengths), jnp.arange(rows * top), side="right").astype(jnp.int32)
    listing = members.reshape(top, rows).T
    listing = listing[jax.random.permutation(jax.random.fold_in(own, 1), rows)]
    rotation = jax.random.randint(jax.random.fold_in(own, 2), (rows, 1), 0, top)
    return jnp.take_along_axis(listing, (jnp.arange(top)[None, :] + rotation) % top, axis=1)


def load_shares(number_of, total, limit, lean, full):
    portions = [(1 << 20) // math.isqrt(standing ** lean) + 1 for standing in range(1, number_of + 1)]
    largest = limit if full else min(limit, max(-(-total // number_of), total * portions[0] // sum(portions)))
    least = 1 if total - largest >= number_of - 1 else 0
    counts, spare = [largest] + [least] * (number_of - 1), total - largest - least * (number_of - 1)
    while spare > 0:
        candidates = [i for i in range(1, number_of) if counts[i] < largest] or [i for i in range(1, number_of) if counts[i] < limit]
        mass, remaining = sum([portions[i] for i in candidates]), spare
        for i in candidates:
            addition = min(limit - counts[i], max(1, remaining * portions[i] // mass), spare)
            counts[i] = counts[i] + addition
            spare = spare - addition
    return np.array(counts)


def scatter_about(stream_key, shape, deviation, limit, shards=(), kind=jnp.bfloat16):
    result = jax.random.normal(stream_key, shape, jnp.float32) * deviation
    if len(shards) > 0:
        result = level_of(stream_key, shape, shards, -0.22, 0.18) * result
    return jnp.clip(result, min=-limit, max=limit).astype(kind)


def setup_inputs(seed: int = 0) -> dict:
    arg_keys = jax.random.split(jax.random.key(seed), 8)
    tokens = scatter_about(arg_keys[0], (TOKENS, D), 1.0, 6.0, ((0, 32),))
    doc_ids = jax.vmap(lambda own: jnp.searchsorted(jnp.cumsum(ragged(own, DOC_DEV, TOK_DEV, DOC_MOST, 1)), jnp.arange(TOK_DEV), side="right"))(jax.random.split(arg_keys[1], SHARDS)).reshape((SHARDS, TOK_DEV)).astype(jnp.int32)
    expert_ids_keys = jax.random.split(jax.random.fold_in(arg_keys[2], 1), TOKENS // TOK_DEV)
    expert_ids_turns = jax.random.permutation(jax.random.fold_in(arg_keys[2], 3), TOKENS // TOK_DEV)
    expert_ids = jax.vmap(lambda own, number: assign_block(jax.random.fold_in(arg_keys[2], 2), own, number, TOK_DEV, EXPERTS, TOP, CAP, 1))(expert_ids_keys, expert_ids_turns).reshape((TOKENS, TOP))
    gate_raw = jnp.clip(jnp.exp(math.log(1.0) - 2.3025851 * jax.random.uniform(arg_keys[3], (TOKENS, TOP), jnp.float32) ** level_of(arg_keys[3], (TOKENS, TOP), ((0, 32),), -0.2, 0.2)), 0.1, 1.0)
    gate_up = scatter_about(arg_keys[4], (EXPERTS, D, 2 * FF), D ** -0.5, 0.125, ((0, 32),))
    down = draw_down(jax.random.fold_in(arg_keys[7], 71), 0)
    bank = draw_bank(jax.random.fold_in(arg_keys[7], 71), 0)
    return {"tokens": tokens, "doc_ids": doc_ids, "expert_ids": expert_ids, "gate_raw": gate_raw, "gate_up": gate_up, "down": down, "bank": bank}


def rms_normed(hidden_rows):
    values = hidden_rows.astype(jnp.float32)
    inverse_rms = lax.rsqrt(lax.optimization_barrier(jnp.mean(values * values, axis=-1, keepdims=True)) + 1e-06)
    return (values * inverse_rms).astype(jnp.bfloat16)

def slot_table(chosen_ids, expert_count):
    chosen = (chosen_ids[:, :, None] == jnp.arange(expert_count, dtype=jnp.int32)[None, None, :]).astype(jnp.int32)
    per_token = lax.optimization_barrier(jnp.sum(chosen, axis=1))
    before = jnp.cumsum(per_token, axis=0) - per_token
    return lax.optimization_barrier(jnp.sum(chosen * before[:, None, :], axis=2)).astype(jnp.int32)

def expert_ffn(rows_in, weights_gu, weights_down):
    hidden_width = weights_down.shape[0]
    gate_and_up = jnp.dot(rows_in, weights_gu, preferred_element_type=jnp.float32)
    hidden = (jax.nn.silu(gate_and_up[:, :hidden_width]) * gate_and_up[:, hidden_width:]).astype(jnp.bfloat16)
    return jnp.dot(hidden, weights_down, preferred_element_type=jnp.float32).astype(jnp.bfloat16)

def reference(tokens, doc_ids, expert_ids, gate_raw, gate_up, down, bank):
    normed = rms_normed(tokens)
    ids_shard = expert_ids.reshape(SHARDS, TOK_DEV, TOP)
    position = jax.vmap(lambda chosen_ids: slot_table(chosen_ids, EXPERTS))(ids_shard)
    shard_of = jnp.broadcast_to(jnp.arange(SHARDS, dtype=jnp.int32)[:, None, None], ids_shard.shape)
    token_of = jnp.broadcast_to(jnp.arange(TOKENS, dtype=jnp.int32).reshape(SHARDS, TOK_DEV)[:, :, None], ids_shard.shape)
    row_table = jnp.full((EXPERTS, SHARDS, CAP), TOKENS, jnp.int32).at[ids_shard, shard_of, position].set(token_of)
    padded = jnp.concatenate([normed, jnp.zeros((1, D), jnp.bfloat16)], axis=0)

    def one_expert(expert_index):
        picked_rows = padded[row_table[expert_index].reshape(-1)]
        return expert_ffn(picked_rows, gate_up[expert_index], down[expert_index])
    outputs = lax.map(one_expert, jnp.arange(EXPERTS, dtype=jnp.int32)).reshape(EXPERTS, SHARDS, CAP, D)
    gate_norm = gate_raw / lax.optimization_barrier(jnp.sum(gate_raw, axis=1, keepdims=True))
    gate_shard = gate_norm.reshape(SHARDS, TOK_DEV, TOP)

    def combine_shard(shard_index):
        picked = outputs[ids_shard[shard_index], shard_index, position[shard_index]]
        return lax.optimization_barrier(jnp.sum(picked.astype(jnp.float32) * gate_shard[shard_index][:, :, None], axis=1))
    combined = lax.map(combine_shard, jnp.arange(SHARDS, dtype=jnp.int32))
    layer_out = combined.reshape(TOKENS, D).astype(jnp.bfloat16)
    member = (jnp.arange(DOC_DEV, dtype=jnp.int32)[None, :, None] == doc_ids[:, None, :]).astype(jnp.float32)
    summed = jnp.einsum('sjt,std->sjd', member, combined, precision=lax.Precision.HIGHEST)
    summed = summed.reshape(DOCS, D)
    pooled = (summed * lax.rsqrt(lax.optimization_barrier(jnp.sum(summed * summed, axis=1, keepdims=True)) + 1e-06)).astype(jnp.bfloat16)
    bank_values = bank.astype(jnp.float32)
    bank_norms = lax.optimization_barrier(jnp.sum(bank_values * bank_values, axis=1))

    def score_shard(doc_block):
        doc_values = doc_block.astype(jnp.float32)
        doc_norms = lax.optimization_barrier(jnp.sum(doc_values * doc_values, axis=1))
        products = jnp.dot(doc_block, bank.T, preferred_element_type=jnp.float32)
        distance = doc_norms[:, None] + bank_norms[None, :] - 2.0 * products
        return lax.optimization_barrier(jnp.min(distance, axis=1))
    scores = lax.map(score_shard, pooled.reshape(SHARDS, DOC_DEV, D)).reshape(DOCS)
    return (layer_out, scores)
```

```python
import functools

import jax
import jax.numpy as jnp
from jax import lax
from jax.experimental import pallas as pl
from jax.experimental.pallas import tpu as pltpu
from jax.sharding import PartitionSpec as P

DOC_DEV = 8
BOTH = ("center", "expert")
CORE, ALONG_X, ALONG_Y = 1, 2, 4
PLANE = (0, ALONG_X, ALONG_Y, ALONG_X | ALONG_Y)


def rms_normed(hidden_rows):
    values = hidden_rows.astype(jnp.float32)
    inverse_rms = lax.rsqrt(jnp.mean(values * values, axis=-1, keepdims=True) + 1e-06)
    return (values * inverse_rms).astype(jnp.bfloat16)


def swap(values, axis, mask):
    size = lax.axis_size(axis)
    return lax.ppermute(values, axis, [(i, i ^ mask) for i in range(size)])


def expert_kernel(capacity, place_ref, gates_ref, *refs):
    blocks = refs[:8]
    gate_up_hbm, down_hbm, own_hbm, other_hbm = refs[8:12]
    rows_in, gate_up, down, picked, hidden, scaled, rows_out, choice = refs[12:20]
    in_sem, weight_sem, out_sem = refs[20:]
    tok_count, model_width = blocks[0].shape
    hidden_width = down_hbm.shape[0]
    tile = 256
    hidden_tiles, model_tiles = hidden_width // tile, model_width // tile

    in_copies = [
        pltpu.make_async_copy(blocks[j], rows_in.at[j], in_sem.at[j]) for j in range(8)
    ]
    weight_copies = [
        pltpu.make_async_copy(gate_up_hbm, gate_up, weight_sem.at[0]),
        pltpu.make_async_copy(down_hbm, down, weight_sem.at[1]),
    ]
    for copy in in_copies + weight_copies:
        copy.start()

    gates = jnp.concatenate([gates_ref[pl.ds(place_ref[j], 1), :] for j in range(8)], axis=0)
    named = gates != 0.0
    before = (
        lax.broadcasted_iota(jnp.int32, (tok_count, tok_count), 0)
        < lax.broadcasted_iota(jnp.int32, (tok_count, tok_count), 1)
    ).astype(jnp.bfloat16)
    slot = jnp.dot(named.astype(jnp.bfloat16), before, preferred_element_type=jnp.float32)
    slot = jnp.where(named, slot, -1.0)
    slot_row = lax.broadcasted_iota(jnp.int32, (capacity, tok_count), 0).astype(jnp.float32)
    gate_columns = []
    for j in range(8):
        hit = slot_row == slot[j : j + 1, :]
        gate_columns.append(
            jnp.sum(jnp.where(hit, gates[j : j + 1, :], 0.0), axis=1, keepdims=True)
        )
        choice[j] = hit.astype(jnp.bfloat16)
    gate_column = jnp.concatenate(gate_columns, axis=0)

    for j in range(8):
        in_copies[j].wait()
        picked[pl.ds(j * capacity, capacity), :] = jnp.dot(
            choice[j], rows_in[j], preferred_element_type=jnp.float32
        ).astype(jnp.bfloat16)

    weight_copies[0].wait()

    @pl.loop(0, hidden_tiles)
    def _(step):
        at = pl.multiple_of(step * tile, tile)
        gate = jnp.dot(
            picked[...], gate_up[:, pl.ds(at, tile)], preferred_element_type=jnp.float32
        )
        up = jnp.dot(
            picked[...],
            gate_up[:, pl.ds(pl.multiple_of(at + hidden_width, tile), tile)],
            preferred_element_type=jnp.float32,
        )
        hidden[:, pl.ds(at, tile)] = (gate / (1.0 + jnp.exp(-gate)) * up).astype(jnp.bfloat16)

    weight_copies[1].wait()

    @pl.loop(0, model_tiles)
    def _(step):
        at = pl.multiple_of(step * tile, tile)
        result = jnp.dot(
            hidden[...], down[:, pl.ds(at, tile)], preferred_element_type=jnp.float32
        )
        scaled[:, pl.ds(at, tile)] = (result * gate_column).astype(jnp.bfloat16)

    out_copies = []
    for j in (4, 5, 6, 7, 0, 1, 2, 3):
        rows_out[j] = lax.dot_general(
            choice[j],
            scaled[pl.ds(j * capacity, capacity), :],
            (((0,), (0,)), ((), ())),
            preferred_element_type=jnp.float32,
        ).astype(jnp.bfloat16)
        target = own_hbm.at[j] if j < 4 else other_hbm.at[j - 4]
        copy = pltpu.make_async_copy(rows_out.at[j], target, out_sem.at[j])
        copy.start()
        out_copies.append(copy)
    for copy in out_copies:
        copy.wait()


def expert_part(capacity, place, gates, blocks, weights_gu, weights_down):
    tok_count, model_width = blocks[0].shape
    hidden_width = weights_down.shape[0]
    rows = 8 * capacity
    bf16 = jnp.bfloat16
    out = jax.ShapeDtypeStruct((4, tok_count, model_width), bf16)
    anywhere = pl.BlockSpec(memory_space=pl.ANY)
    return pl.pallas_call(
        functools.partial(expert_kernel, capacity),
        out_shape=(out, out),
        in_specs=[
            pl.BlockSpec(memory_space=pltpu.SMEM),
            pl.BlockSpec(memory_space=pltpu.VMEM),
        ]
        + [anywhere] * 10,
        out_specs=(anywhere, anywhere),
        scratch_shapes=[
            pltpu.VMEM((8, tok_count, model_width), bf16),
            pltpu.VMEM(weights_gu.shape, bf16),
            pltpu.VMEM(weights_down.shape, bf16),
            pltpu.VMEM((rows, model_width), bf16),
            pltpu.VMEM((rows, hidden_width), bf16),
            pltpu.VMEM((rows, model_width), bf16),
            pltpu.VMEM((8, tok_count, model_width), bf16),
            pltpu.VMEM((8, capacity, tok_count), bf16),
            pltpu.SemaphoreType.DMA((8,)),
            pltpu.SemaphoreType.DMA((2,)),
            pltpu.SemaphoreType.DMA((8,)),
        ],
        compiler_params=pltpu.CompilerParams(vmem_limit_bytes=40 * 1024 * 1024),
        cost_estimate=pl.CostEstimate(
            flops=6 * rows * model_width * hidden_width + 4 * rows * tok_count * model_width,
            bytes_accessed=2 * (3 * model_width * hidden_width + 16 * tok_count * model_width),
            transcendentals=rows * hidden_width,
        ),
        name="expert_part",
    )(place, gates, *blocks, weights_gu, weights_down)


def added(*terms):
    total = terms[0].astype(jnp.float32)
    for term in terms[1:]:
        total = total + term.astype(jnp.float32)
    return total


def gathered_layer(normed, gate_table, weights_gu, weights_down, capacity):
    expert_axis = lax.axis_size("expert")
    center_at, expert_at = lax.axis_index("center"), lax.axis_index("expert")
    expert_count = gate_table.shape[0]
    me = center_at * expert_axis + expert_at
    gates = lax.all_gather(gate_table, BOTH, axis=0, tiled=True)
    order = range(expert_axis)
    lines = [normed] + [swap(normed, "expert", step) for step in order[1:]]
    results = []
    for step in order:
        block = lines[step]
        from_x = swap(block, "center", ALONG_X)
        from_y = swap(block, "center", ALONG_Y)
        if step % 2 == 0:
            from_xy = swap(from_y, "center", ALONG_X)
        else:
            from_xy = swap(from_x, "center", ALONG_Y)
        own = [block, from_x, from_y, from_xy]
        other = [swap(part, "center", CORE) for part in own]
        places = [
            ((center_at ^ mask) * expert_axis + (expert_at ^ step)) * expert_count + me
            for mask in [m for m in PLANE] + [m ^ CORE for m in PLANE]
        ]
        results.append(
            expert_part(
                capacity,
                jnp.stack(places).astype(jnp.int32),
                gates,
                own + other,
                weights_gu,
                weights_down,
            )
        )
    sums = []
    bf16 = jnp.bfloat16
    for step in order:
        own, other = results[step]
        back = swap(other, "center", CORE)
        corner = added(own[3], back[3]).astype(bf16)
        if step % 2 == 0:
            part_x = added(own[1], back[1]).astype(bf16)
            part_y = added(own[2], back[2], swap(corner, "center", ALONG_X)).astype(bf16)
        else:
            part_x = added(own[1], back[1], swap(corner, "center", ALONG_Y)).astype(bf16)
            part_y = added(own[2], back[2]).astype(bf16)
        mine = added(
            own[0], back[0], swap(part_x, "center", ALONG_X), swap(part_y, "center", ALONG_Y)
        )
        sums.append(mine if step == 0 else swap(mine.astype(bf16), "expert", step))
    return added(*sums)


def slot_table(chosen_ids, expert_count):
    chosen = (
        chosen_ids[:, :, None] == jnp.arange(expert_count, dtype=jnp.int32)[None, None, :]
    ).astype(jnp.int32)
    per_token = jnp.sum(chosen, axis=1)
    before = jnp.cumsum(per_token, axis=0) - per_token
    return jnp.sum(chosen * before[:, None, :], axis=2)


def expert_ffn(rows_in, weights_gu, weights_down):
    model_width = rows_in.shape[-1]
    flat_rows = rows_in.reshape(-1, model_width)
    hidden_width = weights_down.shape[0]
    gate_and_up = jnp.dot(flat_rows, weights_gu, preferred_element_type=jnp.float32)
    hidden = (jax.nn.silu(gate_and_up[:, :hidden_width]) * gate_and_up[:, hidden_width:]).astype(
        jnp.bfloat16
    )
    result = jnp.dot(hidden, weights_down, preferred_element_type=jnp.float32).astype(jnp.bfloat16)
    return result.reshape(rows_in.shape)


def exchanged_layer(normed, expert_ids, gate_norm, weights_gu, weights_down, capacity):
    tok_count, top_count = expert_ids.shape
    model_width = normed.shape[1]
    expert_count = lax.axis_size("center") * lax.axis_size("expert")
    position = slot_table(expert_ids, expert_count)
    target = (expert_ids * capacity + position).reshape(-1)
    repeated = jnp.broadcast_to(normed[:, None, :], (tok_count, top_count, model_width)).reshape(
        -1, model_width
    )
    send_buffer = (
        jnp.zeros((expert_count * capacity, model_width), jnp.bfloat16).at[target].set(repeated)
    )
    send_buffer = send_buffer.reshape(expert_count, capacity, model_width)
    computed = expert_ffn(
        lax.all_to_all(send_buffer, BOTH, split_axis=0, concat_axis=0, tiled=True),
        weights_gu,
        weights_down,
    )
    returned = lax.all_to_all(computed, BOTH, split_axis=0, concat_axis=0, tiled=True)
    returned = returned.reshape(expert_count * capacity, model_width)
    gathered = returned[target].reshape(tok_count, top_count, model_width)
    return jnp.sum(gathered.astype(jnp.float32) * gate_norm[:, :, None], axis=1)


def local(tokens, doc_ids, expert_ids, gate_raw, gate_up, down, bank):
    center_count = lax.axis_size("center")
    expert_axis = lax.axis_size("expert")
    expert_count = center_count * expert_axis
    tok_count, top_count = expert_ids.shape
    capacity = min(tok_count, 2 * tok_count * top_count // expert_count)
    normed = rms_normed(tokens)
    gate_norm = gate_raw / jnp.sum(gate_raw, axis=1, keepdims=True)
    weights_gu = gate_up[0]
    weights_down = down[0]
    if center_count == 8 and expert_axis == 4:
        named = expert_ids[:, :, None] == jnp.arange(expert_count, dtype=jnp.int32)[None, None, :]
        gate_table = jnp.sum(jnp.where(named, gate_norm[:, :, None], 0.0), axis=1).T
        combined = gathered_layer(normed, gate_table, weights_gu, weights_down, capacity)
    else:
        combined = exchanged_layer(
            normed, expert_ids, gate_norm, weights_gu, weights_down, capacity
        )
    layer_out = combined.astype(jnp.bfloat16)
    member = (jnp.arange(DOC_DEV, dtype=jnp.int32)[:, None] == doc_ids[0][None, :]).astype(
        jnp.float32
    )
    summed = jnp.dot(
        member, combined, precision=lax.Precision.HIGHEST, preferred_element_type=jnp.float32
    )
    pooled = (summed * lax.rsqrt(jnp.sum(summed * summed, axis=1, keepdims=True) + 1e-06)).astype(
        jnp.bfloat16
    )
    bank_values = bank.astype(jnp.float32)
    bank_norms = jnp.sum(bank_values * bank_values, axis=1)
    shard_part = lax.all_gather(pooled, "center", axis=0, tiled=True)
    doc_values = shard_part.astype(jnp.float32)
    doc_norms = jnp.sum(doc_values * doc_values, axis=1)
    products = lax.dot_general(
        shard_part, bank, (((1,), (1,)), ((), ())), preferred_element_type=jnp.float32
    )
    distance = doc_norms[:, None] + bank_norms[None, :] - 2.0 * products
    nearest = jnp.min(distance, axis=1)
    merged = lax.pmin(nearest, "center")
    own_scores = lax.dynamic_slice_in_dim(merged, lax.axis_index("center") * DOC_DEV, DOC_DEV)
    return (layer_out, own_scores)


def solution(mesh):
    return jax.shard_map(
        local,
        mesh=mesh,
        in_specs=(
            P(BOTH, None),
            P(BOTH, None),
            P(BOTH, None),
            P(BOTH, None),
            P(BOTH, None, None),
            P(BOTH, None, None),
            P("center", None),
        ),
        out_specs=(P(BOTH, None), P(BOTH)),
        check_vma=False,
    )
```

```python
import functools

import jax
import jax.numpy as jnp
from jax import lax
from jax.experimental import pallas as pl
from jax.experimental.pallas import tpu as pltpu
from jax.sharding import PartitionSpec as P

DOC_DEV = 8
BOTH = ("center", "expert")
CORE, ALONG_X, ALONG_Y = 1, 2, 4
LANES = 128


def rms_normed(hidden_rows):
    values = hidden_rows.astype(jnp.float32)
    inverse_rms = lax.rsqrt(jnp.mean(values * values, axis=-1, keepdims=True) + 1e-06)
    return (values * inverse_rms).astype(jnp.bfloat16)


KERNEL = pltpu.CompilerParams(vmem_limit_bytes=24 * 1024 * 1024)
ANYWHERE = pl.BlockSpec(memory_space=pltpu.HBM)
IN_VMEM = pl.BlockSpec(memory_space=pltpu.VMEM)
BESIDE = pl.CostEstimate(flops=1000, bytes_accessed=1000, transcendentals=0)
IN_SMEM = pl.BlockSpec(memory_space=pltpu.SMEM)
BF16 = jnp.bfloat16


def gate_lanes(shape, expert, expert_count):
    lane = lax.broadcasted_iota(jnp.int32, shape, len(shape) - 1)
    return (
        (lane == expert) | (lane == expert + expert_count) | (lane == expert + 2 * expert_count)
    )


def pick_kernel(capacity, expert_count, who_ref, *refs):
    count = len(refs) - 9
    blocks = refs[:count]
    mine_hbm, other_hbm, choice_hbm, rows_in, mine, other, choice, in_sem, out_sem = refs[count:]
    tok_count = blocks[0].shape[0]
    model_width = blocks[0].shape[1] - LANES
    in_copies = [
        pltpu.make_async_copy(blocks[j], rows_in.at[j], in_sem.at[j]) for j in range(count)
    ]
    for copy in in_copies:
        copy.start()
    row = lax.broadcasted_iota(jnp.int32, (8, LANES), 0)
    asked = jnp.where(
        row == 0,
        gate_lanes((8, LANES), who_ref[0], expert_count).astype(jnp.float32),
        gate_lanes((8, LANES), who_ref[1], expert_count).astype(jnp.float32),
    ).astype(BF16)
    before = (
        lax.broadcasted_iota(jnp.int32, (tok_count, tok_count), 0)
        < lax.broadcasted_iota(jnp.int32, (tok_count, tok_count), 1)
    ).astype(jnp.float32).astype(BF16)
    slot_row = lax.broadcasted_iota(jnp.int32, (2 * capacity, tok_count), 0)
    first_half = slot_row < capacity
    slot_row = slot_row.astype(jnp.float32)
    out_copies = []
    for copy in in_copies:
        copy.wait()
    tails = rows_in[:, :, pl.ds(model_width, LANES)].reshape(count * tok_count, LANES)
    gates = lax.dot_general(
        asked, tails, (((1,), (1,)), ((), ())), preferred_element_type=jnp.float32
    )
    named = gates != 0.0
    ones = named.astype(jnp.float32).astype(BF16)
    for j in range(count):
        at = j * tok_count
        slot = jnp.dot(ones[:, at : at + tok_count], before, preferred_element_type=jnp.float32)
        slot = jnp.where(named[:, at : at + tok_count], slot, -1.0 - 2.0 * capacity)
        slot = jnp.where(first_half, slot[0:1, :], slot[1:2, :] + float(capacity))
        choice[j] = (slot == slot_row).astype(jnp.float32).astype(BF16)
    for j in range(count):
        picked = jnp.dot(choice[j], rows_in[j], preferred_element_type=jnp.float32).astype(BF16)
        here = pl.ds(j * capacity, capacity)
        mine[here, :] = picked[:capacity]
        other[here, :] = picked[capacity:]
        for at, (source, target) in enumerate(
            (
                (other.at[here], other_hbm.at[here]),
                (mine.at[here], mine_hbm.at[here]),
                (choice.at[j], choice_hbm.at[j]),
            )
        ):
            copy = pltpu.make_async_copy(source, target, out_sem.at[at, j])
            copy.start()
            out_copies.append(copy)
    for copy in out_copies:
        copy.wait()


def pick(capacity, expert_count, who, blocks):
    count, tok_count, row_width = len(blocks), *blocks[0].shape
    picked = (count * capacity, row_width)
    choice = (count, 2 * capacity, tok_count)
    return pl.pallas_call(
        functools.partial(pick_kernel, capacity, expert_count),
        out_shape=[jax.ShapeDtypeStruct(shape, BF16) for shape in (picked, picked, choice)],
        in_specs=[IN_SMEM] + [ANYWHERE] * count,
        out_specs=[ANYWHERE] * 3,
        scratch_shapes=[
            pltpu.VMEM((count, tok_count, row_width), BF16),
            pltpu.VMEM(picked, BF16),
            pltpu.VMEM(picked, BF16),
            pltpu.VMEM(choice, BF16),
            pltpu.SemaphoreType.DMA((count,)),
            pltpu.SemaphoreType.DMA((3, count)),
        ],
        compiler_params=KERNEL,
        cost_estimate=BESIDE,
        name="pick",
    )(who, *blocks)


def expert_kernel(expert_count, groups, who_ref, *refs):
    parts = refs[: 2 * groups]
    gate_up, down = refs[2 * groups : 2 * groups + 2]
    outs = refs[2 * groups + 2 : 4 * groups + 2]
    rows, hidden, result, in_sem, out_sem = refs[4 * groups + 2 :]
    row_count = rows.shape[0]
    hidden_width, model_width = down.shape
    tile = 256
    hidden_tiles, model_tiles = hidden_width // tile, model_width // tile
    starts = [0]
    for part in parts:
        starts.append(starts[-1] + part.shape[0])
    in_copies = [
        pltpu.make_async_copy(part, rows.at[pl.ds(starts[i], part.shape[0])], in_sem.at[i])
        for i, part in enumerate(parts)
    ]
    for copy in in_copies:
        copy.start()
    for copy in in_copies:
        copy.wait()
    tail = rows[:, pl.ds(model_width, LANES)].astype(jnp.float32)
    gate_column = jnp.sum(
        jnp.where(gate_lanes((row_count, LANES), who_ref[0], expert_count), tail, 0.0),
        axis=1,
        keepdims=True,
    )
    for step in range(hidden_tiles):
        at = step * tile
        values = rows[:, pl.ds(0, model_width)]
        gate = jnp.dot(values, gate_up[:, pl.ds(at, tile)], preferred_element_type=jnp.float32)
        up = jnp.dot(
            values,
            gate_up[:, pl.ds(at + hidden_width, tile)],
            preferred_element_type=jnp.float32,
        )
        hidden[:, pl.ds(at, tile)] = (gate / (1.0 + jnp.exp(-gate)) * up).astype(BF16)
    for step in range(model_tiles):
        at = step * tile
        product = jnp.dot(
            hidden[...], down[:, pl.ds(at, tile)], preferred_element_type=jnp.float32
        )
        result[:, pl.ds(at, tile)] = (product * gate_column).astype(BF16)
    out_copies = [
        pltpu.make_async_copy(result.at[pl.ds(starts[i], out.shape[0])], out, out_sem.at[i])
        for i, out in enumerate(outs)
    ]
    for copy in out_copies:
        copy.start()
    for copy in out_copies:
        copy.wait()


def expert_rows(expert_count, who, parts, weights_gu, weights_down):
    row_width = parts[0].shape[1]
    hidden_width, model_width = weights_down.shape
    rows = sum(part.shape[0] for part in parts)
    outs = [jax.ShapeDtypeStruct((part.shape[0], model_width), BF16) for part in parts]
    return pl.pallas_call(
        functools.partial(expert_kernel, expert_count, len(parts) // 2),
        out_shape=outs,
        in_specs=[IN_SMEM] + [ANYWHERE] * len(parts) + [IN_VMEM] * 2,
        out_specs=[ANYWHERE] * len(parts),
        scratch_shapes=[
            pltpu.VMEM((rows, row_width), BF16),
            pltpu.VMEM((rows, hidden_width), BF16),
            pltpu.VMEM((rows, model_width), BF16),
            pltpu.SemaphoreType.DMA((len(parts),)),
            pltpu.SemaphoreType.DMA((len(parts),)),
        ],
        compiler_params=KERNEL,
        cost_estimate=BESIDE,
        name="expert_rows",
    )(who, *parts, weights_gu, weights_down)


def put_kernel(choice_hbm, mine_hbm, other_hbm, *refs):
    count, rows_two, _ = choice_hbm.shape
    capacity = rows_two // 2
    outs = refs[:count]
    choice, rows, out, in_sem, out_sem = refs[count:]
    copies, out_copies = [], []
    for j in range(count):
        here = pl.ds(j * capacity, capacity)
        copies.append(
            [
                pltpu.make_async_copy(choice_hbm.at[j], choice.at[j], in_sem.at[0, j]),
                pltpu.make_async_copy(
                    mine_hbm.at[here], rows.at[j, pl.ds(0, capacity)], in_sem.at[1, j]
                ),
                pltpu.make_async_copy(
                    other_hbm.at[here], rows.at[j, pl.ds(capacity, capacity)], in_sem.at[2, j]
                ),
            ]
        )
        for copy in copies[-1]:
            copy.start()
    for j in range(count):
        for copy in copies[j]:
            copy.wait()
        out[j] = lax.dot_general(
            choice[j], rows[j], (((0,), (0,)), ((), ())), preferred_element_type=jnp.float32
        ).astype(BF16)
        copy = pltpu.make_async_copy(out.at[j], outs[j], out_sem.at[j])
        copy.start()
        out_copies.append(copy)
    for copy in out_copies:
        copy.wait()


def put(choice, mine, other):
    count, rows_two, tok_count = choice.shape
    model_width = mine.shape[1]
    return pl.pallas_call(
        put_kernel,
        out_shape=[jax.ShapeDtypeStruct((tok_count, model_width), BF16)] * count,
        in_specs=[ANYWHERE] * 3,
        out_specs=[ANYWHERE] * count,
        scratch_shapes=[
            pltpu.VMEM(choice.shape, BF16),
            pltpu.VMEM((count, rows_two, model_width), BF16),
            pltpu.VMEM((count, tok_count, model_width), BF16),
            pltpu.SemaphoreType.DMA((3, count)),
            pltpu.SemaphoreType.DMA((count,)),
        ],
        compiler_params=KERNEL,
        cost_estimate=BESIDE,
        name="put",
    )(choice, mine, other)


def added(*terms):
    total = terms[0].astype(jnp.float32)
    for term in terms[1:]:
        total = total + term.astype(jnp.float32)
    return total


def in_three(values):
    first = values.astype(jnp.bfloat16)
    rest = values - first.astype(jnp.float32)
    second = rest.astype(jnp.bfloat16)
    third = (rest - second.astype(jnp.float32)).astype(jnp.bfloat16)
    return [first, second, third]


SWAP_X = ("center", tuple((i, i ^ ALONG_X) for i in range(8)))
SWAP_Y = ("center", tuple((i, i ^ ALONG_Y) for i in range(8)))
SWAP_CORE = ("center", tuple((i, i ^ CORE) for i in range(8)))
SWAP_Z = ("expert", ((0, 1), (1, 0), (2, 3), (3, 2)))
MIDDLE = ("expert", ((1, 2), (2, 1)))
OUTWARD = ("expert", ((1, 0), (2, 3)))
INWARD = ("expert", ((0, 1), (3, 2)))


def at_once(*sends, behind=()):
    values = [value for _, value in sends]
    if len(behind) > 0:
        held = lax.optimization_barrier((tuple(values), tuple(behind)))
        values = held[0]
    return [lax.ppermute(value, way[0], way[1]) for (way, _), value in zip(sends, values)]


def gathered_layer(rows, who, weights_gu, weights_down, capacity, expert_count, beside):
    def picked(*blocks):
        return pick(capacity, expert_count, who, blocks)

    def crossed(values):
        return at_once((SWAP_CORE, values))[0]

    def worked(*groups):
        parts = [part for mine, other, _ in groups for part in (mine, other)]
        done = expert_rows(expert_count, who, parts, weights_gu, weights_down)
        return [(groups[i][2], done[2 * i], done[2 * i + 1]) for i in range(len(groups))]

    b0 = rows
    bx0, by0, b1, c2 = at_once((SWAP_X, b0), (SWAP_Y, b0), (SWAP_Z, b0), (MIDDLE, b0))
    d0, by1, o2, c3 = at_once(
        (SWAP_X, by0), (SWAP_Y, b1), (OUTWARD, c2), (MIDDLE, b1),
        behind=(bx0, by0, b1, c2),
    )
    mine, other, choice = picked(b0, bx0, by0, b1)
    first = (mine, crossed(other), choice)
    b2 = c2 + o2
    bx2, by2, o3 = at_once(
        (SWAP_X, b2), (SWAP_Y, b2), (OUTWARD, c3), behind=(d0, by1, c3, mine, beside)
    )
    mine, other, choice = picked(d0, by1, b2)
    second = (mine, crossed(other), choice)
    b3 = c3 + o3
    bx3, by3, bx1 = at_once(
        (SWAP_X, b3), (SWAP_Y, b3), (SWAP_Z, bx0), behind=(bx2, by2, mine)
    )
    mine, other, choice = picked(bx2, by2, b3)
    third = (mine, crossed(other), choice)
    d2, d3, d1 = at_once(
        (SWAP_X, by2), (SWAP_Y, bx3), (SWAP_Z, d0), behind=(bx3, by3, bx1, mine)
    )
    mine, other, choice = picked(bx3, by3, bx1)
    fourth = (mine, crossed(other), choice)
    first, second = worked(first, second)
    held = lax.optimization_barrier((d1, d2, d3, mine, first[1]))
    mine, other, choice = picked(*held[:3])
    last = (mine, crossed(other), choice)
    (last,) = worked(last)
    last = (last[0], last[1], crossed(last[2]))
    g5 = put(*last)
    rx_y2, ry_x3, rz_d0 = at_once((SWAP_X, g5[1]), (SWAP_Y, g5[2]), (SWAP_Z, g5[0]))
    fourth = (lax.optimization_barrier((fourth[0], last[1]))[0], *fourth[1:])
    (fourth,) = worked(fourth)
    g4 = put(fourth[0], fourth[1], crossed(fourth[2]))
    third = (lax.optimization_barrier((third[0], g4[0]))[0], *third[1:])
    (third,) = worked(third)
    g3 = put(third[0], third[1], crossed(third[2]))
    g2 = put(second[0], second[1], crossed(second[2]))
    g1 = put(first[0], first[1], crossed(first[2]))
    sx3 = added(g4[0], ry_x3).astype(BF16)
    rx_b3, ry_b3, rz_x0 = at_once(
        (SWAP_X, sx3), (SWAP_Y, g4[1]), (SWAP_Z, g4[2]), behind=(rx_y2, rz_d0, g4[0])
    )
    sy2 = added(g3[1], rx_y2).astype(BF16)
    s3 = added(g3[2], rx_b3, ry_b3).astype(BF16)
    rx_b2, ry_b2, in_3 = at_once(
        (SWAP_X, g3[0]), (SWAP_Y, sy2), (INWARD, s3), behind=(rz_x0, g3[0])
    )
    sd0 = added(g2[0], rz_d0).astype(BF16)
    s2 = added(g2[2], rx_b2, ry_b2).astype(BF16)
    rx_y0, ry_b1, in_2, over_3 = at_once(
        (SWAP_X, sd0), (SWAP_Y, g2[1]), (INWARD, s2),
        (MIDDLE, added(s3, in_3).astype(BF16)), behind=(g2[0], rx_b2, ry_b2),
    )
    sx0 = added(g1[1], rz_x0).astype(BF16)
    sy0 = added(g1[2], rx_y0).astype(BF16)
    s1 = added(g1[3], ry_b1, over_3).astype(BF16)
    rx_b0, ry_b0, rz_b0, over_2 = at_once(
        (SWAP_X, sx0), (SWAP_Y, sy0), (SWAP_Z, s1),
        (MIDDLE, added(s2, in_2).astype(BF16)),
    )
    return added(g1[0], rx_b0, ry_b0, rz_b0, over_2)


def slot_table(chosen_ids, expert_count):
    chosen = (
        chosen_ids[:, :, None] == jnp.arange(expert_count, dtype=jnp.int32)[None, None, :]
    ).astype(jnp.int32)
    per_token = jnp.sum(chosen, axis=1)
    before = jnp.cumsum(per_token, axis=0) - per_token
    return jnp.sum(chosen * before[:, None, :], axis=2)


def expert_ffn(rows_in, weights_gu, weights_down):
    model_width = rows_in.shape[-1]
    flat_rows = rows_in.reshape(-1, model_width)
    hidden_width = weights_down.shape[0]
    gate_and_up = jnp.dot(flat_rows, weights_gu, preferred_element_type=jnp.float32)
    hidden = (jax.nn.silu(gate_and_up[:, :hidden_width]) * gate_and_up[:, hidden_width:]).astype(
        jnp.bfloat16
    )
    result = jnp.dot(hidden, weights_down, preferred_element_type=jnp.float32).astype(jnp.bfloat16)
    return result.reshape(rows_in.shape)


def exchanged_layer(normed, expert_ids, gate_norm, weights_gu, weights_down, capacity):
    tok_count, top_count = expert_ids.shape
    model_width = normed.shape[1]
    expert_count = lax.axis_size("center") * lax.axis_size("expert")
    position = slot_table(expert_ids, expert_count)
    target = (expert_ids * capacity + position).reshape(-1)
    repeated = jnp.broadcast_to(normed[:, None, :], (tok_count, top_count, model_width)).reshape(
        -1, model_width
    )
    send_buffer = (
        jnp.zeros((expert_count * capacity, model_width), jnp.bfloat16).at[target].set(repeated)
    )
    send_buffer = send_buffer.reshape(expert_count, capacity, model_width)
    computed = expert_ffn(
        lax.all_to_all(send_buffer, BOTH, split_axis=0, concat_axis=0, tiled=True),
        weights_gu,
        weights_down,
    )
    returned = lax.all_to_all(computed, BOTH, split_axis=0, concat_axis=0, tiled=True)
    returned = returned.reshape(expert_count * capacity, model_width)
    gathered = returned[target].reshape(tok_count, top_count, model_width)
    return jnp.sum(gathered.astype(jnp.float32) * gate_norm[:, :, None], axis=1)


def local(tokens, doc_ids, expert_ids, gate_raw, gate_up, down, bank):
    center_count = lax.axis_size("center")
    expert_axis = lax.axis_size("expert")
    expert_count = center_count * expert_axis
    tok_count, top_count = expert_ids.shape
    capacity = min(tok_count, 2 * tok_count * top_count // expert_count)
    normed = rms_normed(tokens)
    gate_norm = gate_raw / jnp.sum(gate_raw, axis=1, keepdims=True)
    weights_gu = gate_up[0]
    weights_down = down[0]
    bank_values = bank.astype(jnp.float32)
    bank_norms = jnp.sum(bank_values * bank_values, axis=1)
    if center_count == 8 and expert_axis == 4:
        named = expert_ids[:, :, None] == jnp.arange(expert_count, dtype=jnp.int32)[None, None, :]
        gate_table = jnp.sum(jnp.where(named, gate_norm[:, :, None], 0.0), axis=1)
        unused = jnp.zeros((tok_count, LANES - 3 * expert_count), jnp.bfloat16)
        rows = jnp.concatenate([normed, *in_three(gate_table), unused], axis=1)
        center_at, expert_at = lax.axis_index("center"), lax.axis_index("expert")
        who = jnp.stack(
            [center_at * expert_axis + expert_at, (center_at ^ CORE) * expert_axis + expert_at]
        ).astype(jnp.int32)
        combined = gathered_layer(
            rows, who, weights_gu, weights_down, capacity, expert_count, bank_norms
        )
    else:
        combined = exchanged_layer(
            normed, expert_ids, gate_norm, weights_gu, weights_down, capacity
        )
    layer_out = combined.astype(jnp.bfloat16)
    member = (jnp.arange(DOC_DEV, dtype=jnp.int32)[:, None] == doc_ids[0][None, :]).astype(
        jnp.float32
    )
    summed = jnp.dot(
        member, combined, precision=lax.Precision.HIGHEST, preferred_element_type=jnp.float32
    )
    pooled = (summed * lax.rsqrt(jnp.sum(summed * summed, axis=1, keepdims=True) + 1e-06)).astype(
        jnp.bfloat16
    )
    shard_part = lax.all_gather(pooled, "center", axis=0, tiled=True)
    doc_values = shard_part.astype(jnp.float32)
    doc_norms = jnp.sum(doc_values * doc_values, axis=1)
    products = lax.dot_general(
        shard_part, bank, (((1,), (1,)), ((), ())), preferred_element_type=jnp.float32
    )
    distance = doc_norms[:, None] + bank_norms[None, :] - 2.0 * products
    nearest = jnp.min(distance, axis=1)
    if center_count == 8 and expert_axis == 4:
        for way in (SWAP_Y, SWAP_X, SWAP_CORE):
            nearest = jnp.minimum(nearest, at_once((way, nearest))[0])
    else:
        nearest = lax.pmin(nearest, "center")
    own_scores = lax.dynamic_slice_in_dim(nearest, lax.axis_index("center") * DOC_DEV, DOC_DEV)
    return (layer_out, own_scores)


def solution(mesh):
    return jax.shard_map(
        local,
        mesh=mesh,
        in_specs=(
            P(BOTH, None),
            P(BOTH, None),
            P(BOTH, None),
            P(BOTH, None),
            P(BOTH, None, None),
            P(BOTH, None, None),
            P("center", None),
        ),
        out_specs=(P(BOTH, None), P(BOTH)),
        check_vma=False,
    )
```

```python
import functools

import jax
import jax.numpy as jnp
from jax import lax
from jax.experimental import pallas as pl
from jax.experimental.pallas import tpu as pltpu
from jax.sharding import PartitionSpec as P

DOC_DEV = 8
BOTH = ("center", "expert")
CORE, ALONG_X, ALONG_Y = 1, 2, 4
LANES = 128


def rms_normed(hidden_rows):
    values = hidden_rows.astype(jnp.float32)
    inverse_rms = lax.rsqrt(jnp.mean(values * values, axis=-1, keepdims=True) + 1e-06)
    return (values * inverse_rms).astype(jnp.bfloat16)


KERNEL = pltpu.CompilerParams(vmem_limit_bytes=24 * 1024 * 1024)
ANYWHERE = pl.BlockSpec(memory_space=pltpu.HBM)
IN_VMEM = pl.BlockSpec(memory_space=pltpu.VMEM)
BESIDE = pl.CostEstimate(flops=1000, bytes_accessed=1000, transcendentals=0)
IN_SMEM = pl.BlockSpec(memory_space=pltpu.SMEM)
BF16 = jnp.bfloat16


def gate_lanes(shape, expert, expert_count):
    lane = lax.broadcasted_iota(jnp.int32, shape, len(shape) - 1)
    return (
        (lane == expert) | (lane == expert + expert_count) | (lane == expert + 2 * expert_count)
    )


def pick_kernel(capacity, expert_count, who_ref, *refs):
    count = len(refs) - 9
    blocks = refs[:count]
    mine_hbm, other_hbm, choice_hbm, rows_in, mine, other, choice, in_sem, out_sem = refs[count:]
    tok_count = blocks[0].shape[0]
    model_width = blocks[0].shape[1] - LANES
    in_copies = [
        pltpu.make_async_copy(blocks[j], rows_in.at[j], in_sem.at[j]) for j in range(count)
    ]
    for copy in in_copies:
        copy.start()
    row = lax.broadcasted_iota(jnp.int32, (8, LANES), 0)
    asked = jnp.where(
        row == 0,
        gate_lanes((8, LANES), who_ref[0], expert_count).astype(jnp.float32),
        gate_lanes((8, LANES), who_ref[1], expert_count).astype(jnp.float32),
    ).astype(BF16)
    before = (
        lax.broadcasted_iota(jnp.int32, (tok_count, tok_count), 0)
        < lax.broadcasted_iota(jnp.int32, (tok_count, tok_count), 1)
    ).astype(jnp.float32).astype(BF16)
    slot_row = lax.broadcasted_iota(jnp.int32, (2 * capacity, tok_count), 0)
    first_half = slot_row < capacity
    slot_row = slot_row.astype(jnp.float32)
    out_copies = []
    for copy in in_copies:
        copy.wait()
    tails = rows_in[:, :, pl.ds(model_width, LANES)].reshape(count * tok_count, LANES)
    gates = lax.dot_general(
        asked, tails, (((1,), (1,)), ((), ())), preferred_element_type=jnp.float32
    )
    named = gates != 0.0
    ones = named.astype(jnp.float32).astype(BF16)
    for j in range(count):
        at = j * tok_count
        slot = jnp.dot(ones[:, at : at + tok_count], before, preferred_element_type=jnp.float32)
        slot = jnp.where(named[:, at : at + tok_count], slot, -1.0 - 2.0 * capacity)
        slot = jnp.where(first_half, slot[0:1, :], slot[1:2, :] + float(capacity))
        choice[j] = (slot == slot_row).astype(jnp.float32).astype(BF16)
    for j in range(count):
        picked = jnp.dot(choice[j], rows_in[j], preferred_element_type=jnp.float32).astype(BF16)
        here = pl.ds(j * capacity, capacity)
        mine[here, :] = picked[:capacity]
        other[here, :] = picked[capacity:]
        for at, (source, target) in enumerate(
            (
                (other.at[here], other_hbm.at[here]),
                (mine.at[here], mine_hbm.at[here]),
                (choice.at[j], choice_hbm.at[j]),
            )
        ):
            copy = pltpu.make_async_copy(source, target, out_sem.at[at, j])
            copy.start()
            out_copies.append(copy)
    for copy in out_copies:
        copy.wait()


def pick(capacity, expert_count, who, blocks):
    count, tok_count, row_width = len(blocks), *blocks[0].shape
    picked = (count * capacity, row_width)
    choice = (count, 2 * capacity, tok_count)
    return pl.pallas_call(
        functools.partial(pick_kernel, capacity, expert_count),
        out_shape=[jax.ShapeDtypeStruct(shape, BF16) for shape in (picked, picked, choice)],
        in_specs=[IN_SMEM] + [ANYWHERE] * count,
        out_specs=[ANYWHERE] * 3,
        scratch_shapes=[
            pltpu.VMEM((count, tok_count, row_width), BF16),
            pltpu.VMEM(picked, BF16),
            pltpu.VMEM(picked, BF16),
            pltpu.VMEM(choice, BF16),
            pltpu.SemaphoreType.DMA((count,)),
            pltpu.SemaphoreType.DMA((3, count)),
        ],
        compiler_params=KERNEL,
        cost_estimate=BESIDE,
        name="pick",
    )(who, *blocks)


def expert_kernel(expert_count, groups, who_ref, *refs):
    parts = refs[: 2 * groups]
    gate_up, down = refs[2 * groups : 2 * groups + 2]
    outs = refs[2 * groups + 2 : 4 * groups + 2]
    rows, hidden, result, in_sem, out_sem = refs[4 * groups + 2 :]
    row_count = rows.shape[0]
    hidden_width, model_width = down.shape
    tile = 256
    hidden_tiles, model_tiles = hidden_width // tile, model_width // tile
    starts = [0]
    for part in parts:
        starts.append(starts[-1] + part.shape[0])
    in_copies = [
        pltpu.make_async_copy(part, rows.at[pl.ds(starts[i], part.shape[0])], in_sem.at[i])
        for i, part in enumerate(parts)
    ]
    for copy in in_copies:
        copy.start()
    for copy in in_copies:
        copy.wait()
    tail = rows[:, pl.ds(model_width, LANES)].astype(jnp.float32)
    gate_column = jnp.sum(
        jnp.where(gate_lanes((row_count, LANES), who_ref[0], expert_count), tail, 0.0),
        axis=1,
        keepdims=True,
    )
    for step in range(hidden_tiles):
        at = step * tile
        values = rows[:, pl.ds(0, model_width)]
        gate = jnp.dot(values, gate_up[:, pl.ds(at, tile)], preferred_element_type=jnp.float32)
        up = jnp.dot(
            values,
            gate_up[:, pl.ds(at + hidden_width, tile)],
            preferred_element_type=jnp.float32,
        )
        hidden[:, pl.ds(at, tile)] = (gate / (1.0 + jnp.exp(-gate)) * up).astype(BF16)
    for step in range(model_tiles):
        at = step * tile
        product = jnp.dot(
            hidden[...], down[:, pl.ds(at, tile)], preferred_element_type=jnp.float32
        )
        result[:, pl.ds(at, tile)] = (product * gate_column).astype(BF16)
    out_copies = [
        pltpu.make_async_copy(result.at[pl.ds(starts[i], out.shape[0])], out, out_sem.at[i])
        for i, out in enumerate(outs)
    ]
    for copy in out_copies:
        copy.start()
    for copy in out_copies:
        copy.wait()


def expert_rows(expert_count, who, parts, weights_gu, weights_down):
    row_width = parts[0].shape[1]
    hidden_width, model_width = weights_down.shape
    rows = sum(part.shape[0] for part in parts)
    outs = [jax.ShapeDtypeStruct((part.shape[0], model_width), BF16) for part in parts]
    return pl.pallas_call(
        functools.partial(expert_kernel, expert_count, len(parts) // 2),
        out_shape=outs,
        in_specs=[IN_SMEM] + [ANYWHERE] * len(parts) + [IN_VMEM] * 2,
        out_specs=[ANYWHERE] * len(parts),
        scratch_shapes=[
            pltpu.VMEM((rows, row_width), BF16),
            pltpu.VMEM((rows, hidden_width), BF16),
            pltpu.VMEM((rows, model_width), BF16),
            pltpu.SemaphoreType.DMA((len(parts),)),
            pltpu.SemaphoreType.DMA((len(parts),)),
        ],
        compiler_params=KERNEL,
        cost_estimate=BESIDE,
        name="expert_rows",
    )(who, *parts, weights_gu, weights_down)


def put_kernel(choice_hbm, mine_hbm, other_hbm, *refs):
    count, rows_two, _ = choice_hbm.shape
    capacity = rows_two // 2
    outs = refs[:count]
    choice, rows, out, in_sem, out_sem = refs[count:]
    copies, out_copies = [], []
    for j in range(count):
        here = pl.ds(j * capacity, capacity)
        copies.append(
            [
                pltpu.make_async_copy(choice_hbm.at[j], choice.at[j], in_sem.at[0, j]),
                pltpu.make_async_copy(
                    mine_hbm.at[here], rows.at[j, pl.ds(0, capacity)], in_sem.at[1, j]
                ),
                pltpu.make_async_copy(
                    other_hbm.at[here], rows.at[j, pl.ds(capacity, capacity)], in_sem.at[2, j]
                ),
            ]
        )
        for copy in copies[-1]:
            copy.start()
    for j in range(count):
        for copy in copies[j]:
            copy.wait()
        out[j] = lax.dot_general(
            choice[j], rows[j], (((0,), (0,)), ((), ())), preferred_element_type=jnp.float32
        ).astype(BF16)
        copy = pltpu.make_async_copy(out.at[j], outs[j], out_sem.at[j])
        copy.start()
        out_copies.append(copy)
    for copy in out_copies:
        copy.wait()


def put(choice, mine, other):
    count, rows_two, tok_count = choice.shape
    model_width = mine.shape[1]
    return pl.pallas_call(
        put_kernel,
        out_shape=[jax.ShapeDtypeStruct((tok_count, model_width), BF16)] * count,
        in_specs=[ANYWHERE] * 3,
        out_specs=[ANYWHERE] * count,
        scratch_shapes=[
            pltpu.VMEM(choice.shape, BF16),
            pltpu.VMEM((count, rows_two, model_width), BF16),
            pltpu.VMEM((count, tok_count, model_width), BF16),
            pltpu.SemaphoreType.DMA((3, count)),
            pltpu.SemaphoreType.DMA((count,)),
        ],
        compiler_params=KERNEL,
        cost_estimate=BESIDE,
        name="put",
    )(choice, mine, other)


def normed_sum(summed):
    return (summed * lax.rsqrt(jnp.sum(summed * summed, axis=1, keepdims=True) + 1e-06)).astype(
        jnp.bfloat16
    )


def added(*terms):
    total = terms[0].astype(jnp.float32)
    for term in terms[1:]:
        total = total + term.astype(jnp.float32)
    return total


def enter_kernel(expert_count, *refs):
    sources, rows_ref, targets, sem = refs[:4], refs[4], refs[5:9], refs[9]
    copies = [
        pltpu.make_async_copy(source, target, sem.at[i])
        for i, (source, target) in enumerate(zip(sources, targets))
    ]
    for copy in copies:
        copy.start()
    tokens_ref, ids_ref, gates_ref, docs_ref = targets
    tok_count, model_width = tokens_ref.shape
    for copy in copies[1:]:
        copy.wait()
    raw = gates_ref[...]
    gates = raw / jnp.sum(raw, axis=0, keepdims=True)
    ids = ids_ref[...]
    lane = lax.broadcasted_iota(jnp.int32, (LANES, tok_count), 0)
    table = jnp.zeros((LANES, tok_count), jnp.float32)
    for term in range(3):
        for choice in range(ids.shape[0]):
            hit = lane == ids[choice : choice + 1, :] + term * expert_count
            table = jnp.where(hit, gates[choice : choice + 1, :], table)
    first = table.astype(BF16).astype(jnp.float32)
    rest = table - first
    second = rest.astype(BF16).astype(jnp.float32)
    table = jnp.where(
        lane < expert_count, first, jnp.where(lane < 2 * expert_count, second, rest - second)
    )
    table = jnp.where(lane == 3 * expert_count, docs_ref[...].astype(jnp.float32), table)
    rows_ref[:, pl.ds(model_width, LANES)] = jnp.transpose(table).astype(BF16)
    copies[0].wait()
    rows_ref[:, pl.ds(0, model_width)] = rms_normed(tokens_ref[...])


def enter(tokens, expert_ids, gate_raw, doc_ids, expert_count):
    tok_count, model_width = tokens.shape
    return pl.pallas_call(
        functools.partial(enter_kernel, expert_count),
        out_shape=jax.ShapeDtypeStruct((tok_count, model_width + LANES), BF16),
        in_specs=[ANYWHERE] * 4,
        out_specs=IN_VMEM,
        scratch_shapes=[
            pltpu.VMEM(operand.shape, operand.dtype)
            for operand in (tokens, expert_ids.T, gate_raw.T, doc_ids)
        ]
        + [pltpu.SemaphoreType.DMA((4,))],
        compiler_params=pltpu.CompilerParams(vmem_limit_bytes=62 * 1024 * 1024),
        cost_estimate=BESIDE,
        name="enter",
    )(tokens, expert_ids.T, gate_raw.T, doc_ids)


def leave_kernel(doc_lane, sizes, *refs):
    refs = list(refs)
    groups, tails = [], []
    for size in sizes:
        groups.append([refs.pop(0) for _ in range(size)])
        tails.append(refs.pop(0))
    blocks, sums = refs[: len(sizes) - 1], refs[len(sizes) - 1 :]
    for i, group in enumerate(groups):
        total = group[0][...]
        if len(group) > 1:
            total = added(*[term[...] for term in group]).astype(BF16)
            blocks[i - 1][...] = total
        lane = lax.broadcasted_iota(jnp.int32, tails[i].shape, 1)
        named = tails[i][...].astype(jnp.float32)
        named = jnp.sum(jnp.where(lane == doc_lane, named, 0.0), axis=1, keepdims=True)
        member = (named == lane.astype(jnp.float32)).astype(jnp.float32).astype(BF16)
        sums[i][...] = lax.dot_general(
            member, total, (((0,), (0,)), ((), ())), preferred_element_type=jnp.float32
        )[:DOC_DEV]


def leave(doc_lane, groups):
    tok_count, model_width = groups[0][0][0].shape
    operands = [ref for blocks, tail in groups for ref in (*blocks, tail)]
    count = len(groups)
    results = pl.pallas_call(
        functools.partial(leave_kernel, doc_lane, [len(blocks) for blocks, _ in groups]),
        out_shape=[jax.ShapeDtypeStruct((tok_count, model_width), BF16)] * (count - 1)
        + [jax.ShapeDtypeStruct((DOC_DEV, model_width), jnp.float32)] * count,
        in_specs=[IN_VMEM] * len(operands),
        out_specs=[IN_VMEM] * (2 * count - 1),
        compiler_params=KERNEL,
        cost_estimate=BESIDE,
        name="leave",
    )(*operands)
    return results[: count - 1], results[count - 1 :]


SWAP_X = ("center", tuple((i, i ^ ALONG_X) for i in range(8)))
SWAP_Y = ("center", tuple((i, i ^ ALONG_Y) for i in range(8)))
SWAP_XY = ("center", tuple((i, i ^ ALONG_X ^ ALONG_Y) for i in range(8)))
SWAP_CORE = ("center", tuple((i, i ^ CORE) for i in range(8)))
SWAP_Z = ("expert", ((0, 1), (1, 0), (2, 3), (3, 2)))
MIDDLE = ("expert", ((1, 2), (2, 1)))
OUTWARD = ("expert", ((1, 0), (2, 3)))
INWARD = ("expert", ((0, 1), (3, 2)))


def at_once(*sends, behind=()):
    values = [value for _, value in sends]
    if len(behind) > 0:
        held = lax.optimization_barrier((tuple(values), tuple(behind)))
        values = held[0]
    return [lax.ppermute(value, way[0], way[1]) for (way, _), value in zip(sends, values)]


def gathered_layer(rows, who, weights_gu, weights_down, capacity, expert_count, beside):
    def picked(*blocks):
        return pick(capacity, expert_count, who, blocks)

    def crossed(values):
        return at_once((SWAP_CORE, values))[0]

    def worked(*groups):
        parts = [part for mine, other, _ in groups for part in (mine, other)]
        done = expert_rows(expert_count, who, parts, weights_gu, weights_down)
        return [(groups[i][2], done[2 * i], done[2 * i + 1]) for i in range(len(groups))]

    b0 = rows
    bx0, by0, b1, c2 = at_once((SWAP_X, b0), (SWAP_Y, b0), (SWAP_Z, b0), (MIDDLE, b0))
    d0, by1, o2, c3 = at_once(
        (SWAP_X, by0), (SWAP_Y, b1), (OUTWARD, c2), (MIDDLE, b1),
        behind=(bx0, by0, b1, c2),
    )
    mine, other, choice = picked(b0, bx0, by0, b1)
    first = (mine, crossed(other), choice)
    b2 = c2 + o2
    bx2, by2, o3 = at_once(
        (SWAP_X, b2), (SWAP_Y, b2), (OUTWARD, c3), behind=(d0, by1, c3, mine, beside)
    )
    mine, other, choice = picked(d0, by1, b2)
    second = (mine, crossed(other), choice)
    b3 = c3 + o3
    bx3, by3, bx1 = at_once(
        (SWAP_X, b3), (SWAP_Y, b3), (SWAP_Z, bx0), behind=(bx2, by2, mine)
    )
    mine, other, choice = picked(bx2, by2, b3)
    third = (mine, crossed(other), choice)
    (first,) = worked(first)
    d2, d3, d1 = at_once(
        (SWAP_X, by2), (SWAP_Y, bx3), (SWAP_Z, d0), behind=(bx3, by3, bx1, mine, first[1])
    )
    mine, other, choice = picked(bx3, by3, bx1)
    fourth = (mine, crossed(other), choice)
    (third,) = worked(third)
    held = lax.optimization_barrier((d1, d2, d3, mine, third[1]))
    mine, other, choice = picked(*held[:3])
    fourth = (lax.optimization_barrier((fourth[0], mine))[0], *fourth[1:])
    (fourth,) = worked(fourth)
    last = (lax.optimization_barrier((mine, fourth[1]))[0], crossed(other), choice)
    (last,) = worked(last)
    g3 = put(*lax.optimization_barrier((third[0], third[1], crossed(third[2]), last[1]))[:3])
    g5 = put(last[0], last[1], lax.optimization_barrier((crossed(last[2]), g3[0]))[0])
    rx_y2, ry_x3, rz_d0 = at_once((SWAP_X, g5[1]), (SWAP_Y, g5[2]), (SWAP_Z, g5[0]))
    crossed_fourth = crossed(fourth[2])
    g4 = put(*lax.optimization_barrier((fourth[0], fourth[1], crossed_fourth, g5[0]))[:3])
    second = (lax.optimization_barrier((second[0], g5[0]))[0], *second[1:])
    (second,) = worked(second)
    g2 = put(second[0], second[1], crossed(second[2]))
    g1 = put(*lax.optimization_barrier((first[0], first[1], crossed(first[2]), g4[0]))[:3])
    sx3 = added(g4[0], ry_x3).astype(BF16)
    rx_b3, ry_b3, rz_x0 = at_once(
        (SWAP_X, sx3), (SWAP_Y, g4[1]), (SWAP_Z, g4[2]), behind=(rx_y2, rz_d0, g4[0], second[1], g1[0])
    )
    sy2 = added(g3[1], rx_y2).astype(BF16)
    s3 = added(g3[2], rx_b3, ry_b3).astype(BF16)
    rx_b2, ry_b2, in_3 = at_once(
        (SWAP_X, g3[0]), (SWAP_Y, sy2), (INWARD, s3), behind=(rz_x0, g2[0])
    )
    sd0 = added(g2[0], rz_d0).astype(BF16)
    s2 = added(g2[2], rx_b2, ry_b2).astype(BF16)
    rx_y0, ry_b1, in_2, over_3 = at_once(
        (SWAP_X, sd0), (SWAP_Y, g2[1]), (INWARD, s2),
        (MIDDLE, added(s3, in_3).astype(BF16)), behind=(rx_b2, ry_b2),
    )
    (sx0, sy0, s1, m2), (sum_own, *sums) = leave(
        3 * expert_count,
        [
            ([g1[0]], rows[:, -LANES:]),
            ([g1[1], rz_x0], bx0[:, -LANES:]),
            ([g1[2], rx_y0], by0[:, -LANES:]),
            ([g1[3], ry_b1, over_3], b1[:, -LANES:]),
            ([s2, in_2], c2[:, -LANES:]),
        ],
    )
    ways = (SWAP_X, SWAP_Y, SWAP_Z, MIDDLE)
    sums = at_once(*zip(ways, sums))
    pooled = normed_sum(added(sum_own, *sums))
    rx_b0, ry_b0, rz_b0, over_2 = at_once(*zip(ways, (sx0, sy0, s1, m2)))
    return added(g1[0], rx_b0, ry_b0, rz_b0, over_2), pooled


def slot_table(chosen_ids, expert_count):
    chosen = (
        chosen_ids[:, :, None] == jnp.arange(expert_count, dtype=jnp.int32)[None, None, :]
    ).astype(jnp.int32)
    per_token = jnp.sum(chosen, axis=1)
    before = jnp.cumsum(per_token, axis=0) - per_token
    return jnp.sum(chosen * before[:, None, :], axis=2)


def expert_ffn(rows_in, weights_gu, weights_down):
    model_width = rows_in.shape[-1]
    flat_rows = rows_in.reshape(-1, model_width)
    hidden_width = weights_down.shape[0]
    gate_and_up = jnp.dot(flat_rows, weights_gu, preferred_element_type=jnp.float32)
    hidden = (jax.nn.silu(gate_and_up[:, :hidden_width]) * gate_and_up[:, hidden_width:]).astype(
        jnp.bfloat16
    )
    result = jnp.dot(hidden, weights_down, preferred_element_type=jnp.float32).astype(jnp.bfloat16)
    return result.reshape(rows_in.shape)


def exchanged_layer(normed, expert_ids, gate_norm, weights_gu, weights_down, capacity):
    tok_count, top_count = expert_ids.shape
    model_width = normed.shape[1]
    expert_count = lax.axis_size("center") * lax.axis_size("expert")
    position = slot_table(expert_ids, expert_count)
    target = (expert_ids * capacity + position).reshape(-1)
    repeated = jnp.broadcast_to(normed[:, None, :], (tok_count, top_count, model_width)).reshape(
        -1, model_width
    )
    send_buffer = (
        jnp.zeros((expert_count * capacity, model_width), jnp.bfloat16).at[target].set(repeated)
    )
    send_buffer = send_buffer.reshape(expert_count, capacity, model_width)
    computed = expert_ffn(
        lax.all_to_all(send_buffer, BOTH, split_axis=0, concat_axis=0, tiled=True),
        weights_gu,
        weights_down,
    )
    returned = lax.all_to_all(computed, BOTH, split_axis=0, concat_axis=0, tiled=True)
    returned = returned.reshape(expert_count * capacity, model_width)
    gathered = returned[target].reshape(tok_count, top_count, model_width)
    return jnp.sum(gathered.astype(jnp.float32) * gate_norm[:, :, None], axis=1)


def local(tokens, doc_ids, expert_ids, gate_raw, gate_up, down, bank):
    center_count = lax.axis_size("center")
    expert_axis = lax.axis_size("expert")
    expert_count = center_count * expert_axis
    tok_count, top_count = expert_ids.shape
    capacity = min(tok_count, 2 * tok_count * top_count // expert_count)
    weights_gu = gate_up[0]
    weights_down = down[0]
    bank_values = bank.astype(jnp.float32)
    bank_norms = jnp.sum(bank_values * bank_values, axis=1)
    if center_count == 8 and expert_axis == 4:
        rows = enter(tokens, expert_ids, gate_raw, doc_ids, expert_count)
        center_at, expert_at = lax.axis_index("center"), lax.axis_index("expert")
        who = jnp.stack(
            [center_at * expert_axis + expert_at, (center_at ^ CORE) * expert_axis + expert_at]
        ).astype(jnp.int32)
        combined, pooled = gathered_layer(
            rows, who, weights_gu, weights_down, capacity, expert_count, bank_norms
        )
    else:
        gate_norm = gate_raw / jnp.sum(gate_raw, axis=1, keepdims=True)
        combined = exchanged_layer(
            rms_normed(tokens), expert_ids, gate_norm, weights_gu, weights_down, capacity
        )
        member = (jnp.arange(DOC_DEV, dtype=jnp.int32)[:, None] == doc_ids[0][None, :]).astype(
            jnp.float32
        )
        summed = jnp.dot(
            member, combined, precision=lax.Precision.HIGHEST, preferred_element_type=jnp.float32
        )
        pooled = normed_sum(summed)
    layer_out = combined.astype(jnp.bfloat16)
    shard_part = lax.all_gather(pooled, "center", axis=0, tiled=True)
    doc_values = shard_part.astype(jnp.float32)
    doc_norms = jnp.sum(doc_values * doc_values, axis=1)
    products = lax.dot_general(
        shard_part, bank, (((1,), (1,)), ((), ())), preferred_element_type=jnp.float32
    )
    distance = doc_norms[:, None] + bank_norms[None, :] - 2.0 * products
    nearest = jnp.min(distance, axis=1)
    if center_count == 8 and expert_axis == 4:
        ways = (SWAP_X, SWAP_Y, SWAP_XY)
        for arrived in at_once(*[(way, nearest) for way in ways], behind=(layer_out,)):
            nearest = jnp.minimum(nearest, arrived)
        nearest = jnp.minimum(nearest, at_once((SWAP_CORE, nearest))[0])
    else:
        nearest = lax.pmin(nearest, "center")
    own_scores = lax.dynamic_slice_in_dim(nearest, lax.axis_index("center") * DOC_DEV, DOC_DEV)
    return (layer_out, own_scores)


def solution(mesh):
    return jax.shard_map(
        local,
        mesh=mesh,
        in_specs=(
            P(BOTH, None),
            P(BOTH, None),
            P(BOTH, None),
            P(BOTH, None),
            P(BOTH, None, None),
            P(BOTH, None, None),
            P("center", None),
        ),
        out_specs=(P(BOTH, None), P(BOTH)),
        check_vma=False,
    )
```

```python
import functools

import jax
import jax.numpy as jnp
from jax import lax
from jax.experimental import pallas as pl
from jax.experimental.pallas import tpu as pltpu
from jax.sharding import PartitionSpec as P

DOC_DEV = 8
BOTH = ("center", "expert")
CORE, ALONG_X, ALONG_Y = 1, 2, 4
LANES = 128


def rms_normed(hidden_rows):
    values = hidden_rows.astype(jnp.float32)
    inverse_rms = lax.rsqrt(jnp.mean(values * values, axis=-1, keepdims=True) + 1e-06)
    return (values * inverse_rms).astype(jnp.bfloat16)


KERNEL = pltpu.CompilerParams(vmem_limit_bytes=24 * 1024 * 1024)
ANYWHERE = pl.BlockSpec(memory_space=pltpu.HBM)
IN_VMEM = pl.BlockSpec(memory_space=pltpu.VMEM)
BESIDE = pl.CostEstimate(flops=1000, bytes_accessed=1000, transcendentals=0)
IN_SMEM = pl.BlockSpec(memory_space=pltpu.SMEM)
BF16 = jnp.bfloat16


def gate_lanes(shape, expert, expert_count):
    lane = lax.broadcasted_iota(jnp.int32, shape, len(shape) - 1)
    return (
        (lane == expert) | (lane == expert + expert_count) | (lane == expert + 2 * expert_count)
    )


def pick_kernel(capacity, expert_count, who_ref, *refs):
    count = len(refs) - 3
    blocks = refs[:count]
    mine, other, choice = refs[count:]
    tok_count = blocks[0].shape[0]
    model_width = blocks[0].shape[1] - LANES
    row = lax.broadcasted_iota(jnp.int32, (8, LANES), 0)
    asked = jnp.where(
        row == 0,
        gate_lanes((8, LANES), who_ref[0], expert_count).astype(jnp.float32),
        gate_lanes((8, LANES), who_ref[1], expert_count).astype(jnp.float32),
    ).astype(BF16)
    before = (
        lax.broadcasted_iota(jnp.int32, (tok_count, tok_count), 0)
        < lax.broadcasted_iota(jnp.int32, (tok_count, tok_count), 1)
    ).astype(jnp.float32).astype(BF16)
    slot_row = lax.broadcasted_iota(jnp.int32, (2 * capacity, tok_count), 0)
    first_half = slot_row < capacity
    slot_row = slot_row.astype(jnp.float32)
    tails = jnp.concatenate([block[:, pl.ds(model_width, LANES)] for block in blocks], axis=0)
    gates = lax.dot_general(
        asked, tails, (((1,), (1,)), ((), ())), preferred_element_type=jnp.float32
    )
    named = gates != 0.0
    ones = named.astype(jnp.float32).astype(BF16)
    for j in range(count):
        at = j * tok_count
        slot = jnp.dot(ones[:, at : at + tok_count], before, preferred_element_type=jnp.float32)
        slot = jnp.where(named[:, at : at + tok_count], slot, -1.0 - 2.0 * capacity)
        slot = jnp.where(first_half, slot[0:1, :], slot[1:2, :] + float(capacity))
        choice[j] = (slot == slot_row).astype(jnp.float32).astype(BF16)
    for j in range(count):
        picked = jnp.dot(choice[j], blocks[j][...], preferred_element_type=jnp.float32).astype(BF16)
        here = pl.ds(j * capacity, capacity)
        mine[here, :] = picked[:capacity]
        other[here, :] = picked[capacity:]


def pick(capacity, expert_count, who, blocks):
    count, tok_count, row_width = len(blocks), *blocks[0].shape
    picked = (count * capacity, row_width)
    choice = (count, 2 * capacity, tok_count)
    return pl.pallas_call(
        functools.partial(pick_kernel, capacity, expert_count),
        out_shape=[jax.ShapeDtypeStruct(shape, BF16) for shape in (picked, picked, choice)],
        in_specs=[IN_SMEM] + [IN_VMEM] * count,
        out_specs=[IN_VMEM] * 3,
        compiler_params=KERNEL,
        cost_estimate=BESIDE,
        name="pick",
    )(who, *blocks)


def expert_kernel(expert_count, groups, who_ref, *refs):
    parts = refs[: 2 * groups]
    gate_up, down = refs[2 * groups : 2 * groups + 2]
    outs = refs[2 * groups + 2 : 4 * groups + 2]
    rows, hidden, in_sem = refs[4 * groups + 2 :]
    row_count = rows.shape[0]
    hidden_width, model_width = down.shape
    tile = 256
    hidden_tiles, model_tiles = hidden_width // tile, model_width // tile
    starts = [0]
    for part in parts:
        starts.append(starts[-1] + part.shape[0])
    in_copies = [
        pltpu.make_async_copy(part, rows.at[pl.ds(starts[i], part.shape[0])], in_sem.at[i])
        for i, part in enumerate(parts)
    ]
    for copy in in_copies:
        copy.start()
    for copy in in_copies:
        copy.wait()
    tail = rows[:, pl.ds(model_width, LANES)].astype(jnp.float32)
    gate_column = jnp.sum(
        jnp.where(gate_lanes((row_count, LANES), who_ref[0], expert_count), tail, 0.0),
        axis=1,
        keepdims=True,
    )
    for step in range(hidden_tiles):
        at = step * tile
        values = rows[:, pl.ds(0, model_width)]
        gate = jnp.dot(values, gate_up[:, pl.ds(at, tile)], preferred_element_type=jnp.float32)
        up = jnp.dot(
            values,
            gate_up[:, pl.ds(at + hidden_width, tile)],
            preferred_element_type=jnp.float32,
        )
        hidden[:, pl.ds(at, tile)] = (gate / (1.0 + jnp.exp(-gate)) * up).astype(BF16)
    for step in range(model_tiles):
        at = step * tile
        product = jnp.dot(
            hidden[...], down[:, pl.ds(at, tile)], preferred_element_type=jnp.float32
        )
        product = (product * gate_column).astype(BF16)
        for i, out in enumerate(outs):
            out[:, pl.ds(at, tile)] = product[starts[i] : starts[i + 1]]


def expert_rows(expert_count, who, parts, weights_gu, weights_down):
    row_width = parts[0].shape[1]
    hidden_width, model_width = weights_down.shape
    rows = sum(part.shape[0] for part in parts)
    outs = [jax.ShapeDtypeStruct((part.shape[0], model_width), BF16) for part in parts]
    return pl.pallas_call(
        functools.partial(expert_kernel, expert_count, len(parts) // 2),
        out_shape=outs,
        in_specs=[IN_SMEM] + [ANYWHERE] * len(parts) + [IN_VMEM] * 2,
        out_specs=[IN_VMEM] * len(parts),
        scratch_shapes=[
            pltpu.VMEM((rows, row_width), BF16),
            pltpu.VMEM((rows, hidden_width), BF16),
            pltpu.SemaphoreType.DMA((len(parts),)),
        ],
        compiler_params=KERNEL,
        cost_estimate=BESIDE,
        name="expert_rows",
    )(who, *parts, weights_gu, weights_down)


def put_kernel(choice, mine, other, *outs):
    capacity = choice.shape[1] // 2
    for j, out in enumerate(outs):
        here = pl.ds(j * capacity, capacity)
        rows = jnp.concatenate([mine[here, :], other[here, :]], axis=0)
        out[...] = lax.dot_general(
            choice[j], rows, (((0,), (0,)), ((), ())), preferred_element_type=jnp.float32
        ).astype(BF16)


def put(choice, mine, other):
    count, _, tok_count = choice.shape
    model_width = mine.shape[1]
    return pl.pallas_call(
        put_kernel,
        out_shape=[jax.ShapeDtypeStruct((tok_count, model_width), BF16)] * count,
        in_specs=[IN_VMEM] * 3,
        out_specs=[IN_VMEM] * count,
        compiler_params=KERNEL,
        cost_estimate=BESIDE,
        name="put",
    )(choice, mine, other)


def normed_sum(summed):
    return (summed * lax.rsqrt(jnp.sum(summed * summed, axis=1, keepdims=True) + 1e-06)).astype(
        jnp.bfloat16
    )


def added(*terms):
    total = terms[0].astype(jnp.float32)
    for term in terms[1:]:
        total = total + term.astype(jnp.float32)
    return total


def enter_kernel(expert_count, *refs):
    sources, rows_ref, targets, sem = refs[:4], refs[4], refs[5:9], refs[9]
    copies = [
        pltpu.make_async_copy(source, target, sem.at[i])
        for i, (source, target) in enumerate(zip(sources, targets))
    ]
    for copy in copies:
        copy.start()
    tokens_ref, ids_ref, gates_ref, docs_ref = targets
    tok_count, model_width = tokens_ref.shape
    for copy in copies[1:]:
        copy.wait()
    raw = gates_ref[...]
    gates = raw / jnp.sum(raw, axis=0, keepdims=True)
    ids = ids_ref[...]
    lane = lax.broadcasted_iota(jnp.int32, (LANES, tok_count), 0)
    table = jnp.zeros((LANES, tok_count), jnp.float32)
    for term in range(3):
        for choice in range(ids.shape[0]):
            hit = lane == ids[choice : choice + 1, :] + term * expert_count
            table = jnp.where(hit, gates[choice : choice + 1, :], table)
    first = table.astype(BF16).astype(jnp.float32)
    rest = table - first
    second = rest.astype(BF16).astype(jnp.float32)
    table = jnp.where(
        lane < expert_count, first, jnp.where(lane < 2 * expert_count, second, rest - second)
    )
    table = jnp.where(lane == 3 * expert_count, docs_ref[...].astype(jnp.float32), table)
    rows_ref[:, pl.ds(model_width, LANES)] = jnp.transpose(table).astype(BF16)
    copies[0].wait()
    rows_ref[:, pl.ds(0, model_width)] = rms_normed(tokens_ref[...])


def enter(tokens, expert_ids, gate_raw, doc_ids, expert_count):
    tok_count, model_width = tokens.shape
    return pl.pallas_call(
        functools.partial(enter_kernel, expert_count),
        out_shape=jax.ShapeDtypeStruct((tok_count, model_width + LANES), BF16),
        in_specs=[ANYWHERE] * 4,
        out_specs=IN_VMEM,
        scratch_shapes=[
            pltpu.VMEM(operand.shape, operand.dtype)
            for operand in (tokens, expert_ids.T, gate_raw.T, doc_ids)
        ]
        + [pltpu.SemaphoreType.DMA((4,))],
        compiler_params=pltpu.CompilerParams(vmem_limit_bytes=62 * 1024 * 1024),
        cost_estimate=BESIDE,
        name="enter",
    )(tokens, expert_ids.T, gate_raw.T, doc_ids)


def leave_kernel(doc_lane, sizes, *refs):
    refs = list(refs)
    groups, tails = [], []
    for size in sizes:
        groups.append([refs.pop(0) for _ in range(size)])
        tails.append(refs.pop(0))
    blocks, sums = refs[: len(sizes) - 1], refs[len(sizes) - 1 :]
    for i, group in enumerate(groups):
        total = group[0][...]
        if len(group) > 1:
            total = added(*[term[...] for term in group]).astype(BF16)
            blocks[i - 1][...] = total
        lane = lax.broadcasted_iota(jnp.int32, tails[i].shape, 1)
        named = tails[i][...].astype(jnp.float32)
        named = jnp.sum(jnp.where(lane == doc_lane, named, 0.0), axis=1, keepdims=True)
        member = (named == lane.astype(jnp.float32)).astype(jnp.float32).astype(BF16)
        sums[i][...] = lax.dot_general(
            member, total, (((0,), (0,)), ((), ())), preferred_element_type=jnp.float32
        )[:DOC_DEV]


def leave(doc_lane, groups):
    tok_count, model_width = groups[0][0][0].shape
    operands = [ref for blocks, tail in groups for ref in (*blocks, tail)]
    count = len(groups)
    results = pl.pallas_call(
        functools.partial(leave_kernel, doc_lane, [len(blocks) for blocks, _ in groups]),
        out_shape=[jax.ShapeDtypeStruct((tok_count, model_width), BF16)] * (count - 1)
        + [jax.ShapeDtypeStruct((DOC_DEV, model_width), jnp.float32)] * count,
        in_specs=[IN_VMEM] * len(operands),
        out_specs=[IN_VMEM] * (2 * count - 1),
        compiler_params=KERNEL,
        cost_estimate=BESIDE,
        name="leave",
    )(*operands)
    return results[: count - 1], results[count - 1 :]


SWAP_X = ("center", tuple((i, i ^ ALONG_X) for i in range(8)))
SWAP_Y = ("center", tuple((i, i ^ ALONG_Y) for i in range(8)))
SWAP_XY = ("center", tuple((i, i ^ ALONG_X ^ ALONG_Y) for i in range(8)))
SWAP_CORE = ("center", tuple((i, i ^ CORE) for i in range(8)))
SWAP_Z = ("expert", ((0, 1), (1, 0), (2, 3), (3, 2)))
MIDDLE = ("expert", ((1, 2), (2, 1)))


def at_once(*sends, behind=()):
    values = [value for _, value in sends]
    if len(behind) > 0:
        held = lax.optimization_barrier((tuple(values), tuple(behind)))
        values = held[0]
    return [lax.ppermute(value, way[0], way[1]) for (way, _), value in zip(sends, values)]


def gathered_layer(rows, who, weights_gu, weights_down, capacity, expert_count, beside):
    def picked(*blocks):
        return pick(capacity, expert_count, who, blocks)

    def crossed(values):
        return at_once((SWAP_CORE, values))[0]

    def worked(*groups):
        parts = [part for mine, other, _ in groups for part in (mine, other)]
        done = expert_rows(expert_count, who, parts, weights_gu, weights_down)
        return [(groups[i][2], done[2 * i], done[2 * i + 1]) for i in range(len(groups))]

    b0 = rows
    bx0, by0, b1, c2 = at_once((SWAP_X, b0), (SWAP_Y, b0), (SWAP_Z, b0), (MIDDLE, b0))
    d0, by1, o2, c3 = at_once(
        (SWAP_X, by0), (SWAP_Y, b1), (SWAP_Z, c2), (MIDDLE, b1),
        behind=(bx0, by0, b1, c2),
    )
    mine, other, choice = picked(b0, bx0, by0, b1)
    first = (mine, crossed(other), choice)
    b2 = c2 + o2
    bx2, by2, o3 = at_once(
        (SWAP_X, b2), (SWAP_Y, b2), (SWAP_Z, c3), behind=(d0, by1, c3, mine, beside)
    )
    mine, other, choice = picked(d0, by1, b2)
    second = (mine, crossed(other), choice)
    b3 = c3 + o3
    bx3, by3, bx1 = at_once(
        (SWAP_X, b3), (SWAP_Y, b3), (SWAP_Z, bx0), behind=(bx2, by2, mine)
    )
    mine, other, choice = picked(bx2, by2, b3)
    third = (mine, crossed(other), choice)
    (first,) = worked(first)
    d2, d3, d1 = at_once(
        (SWAP_X, by2), (SWAP_Y, bx3), (SWAP_Z, d0), behind=(bx3, by3, bx1, mine, first[1])
    )
    mine, other, choice = picked(bx3, by3, bx1)
    fourth = (mine, crossed(other), choice)
    (third,) = worked(third)
    held = lax.optimization_barrier((d1, d2, d3, mine, third[1]))
    mine, other, choice = picked(*held[:3])
    fourth = (lax.optimization_barrier((fourth[0], mine))[0], *fourth[1:])
    (fourth,) = worked(fourth)
    last = (lax.optimization_barrier((mine, fourth[1]))[0], crossed(other), choice)
    (last,) = worked(last)
    g3 = put(*lax.optimization_barrier((third[0], third[1], crossed(third[2]), last[1]))[:3])
    g5 = put(last[0], last[1], lax.optimization_barrier((crossed(last[2]), g3[0]))[0])
    rx_y2, ry_x3, rz_d0 = at_once((SWAP_X, g5[1]), (SWAP_Y, g5[2]), (SWAP_Z, g5[0]))
    crossed_fourth = crossed(fourth[2])
    g4 = put(*lax.optimization_barrier((fourth[0], fourth[1], crossed_fourth, g5[0]))[:3])
    second = (lax.optimization_barrier((second[0], g5[0]))[0], *second[1:])
    (second,) = worked(second)
    g2 = put(second[0], second[1], crossed(second[2]))
    g1 = put(*lax.optimization_barrier((first[0], first[1], crossed(first[2]), g4[0]))[:3])
    sx3 = added(g4[0], ry_x3).astype(BF16)
    rx_b3, ry_b3, rz_x0 = at_once(
        (SWAP_X, sx3), (SWAP_Y, g4[1]), (SWAP_Z, g4[2]), behind=(rx_y2, rz_d0, g4[0], second[1], g1[0])
    )
    sy2 = added(g3[1], rx_y2).astype(BF16)
    s3 = added(g3[2], rx_b3, ry_b3).astype(BF16)
    rx_b2, ry_b2, in_3 = at_once(
        (SWAP_X, g3[0]), (SWAP_Y, sy2), (SWAP_Z, s3), behind=(rz_x0, g2[0])
    )
    sd0 = added(g2[0], rz_d0).astype(BF16)
    s2 = added(g2[2], rx_b2, ry_b2).astype(BF16)
    rx_y0, ry_b1, in_2, over_3 = at_once(
        (SWAP_X, sd0), (SWAP_Y, g2[1]), (SWAP_Z, s2),
        (MIDDLE, added(s3, in_3).astype(BF16)), behind=(rx_b2, ry_b2),
    )
    (sx0, sy0, s1, m2), (sum_own, *sums) = leave(
        3 * expert_count,
        [
            ([g1[0]], rows[:, -LANES:]),
            ([g1[1], rz_x0], bx0[:, -LANES:]),
            ([g1[2], rx_y0], by0[:, -LANES:]),
            ([g1[3], ry_b1, over_3], b1[:, -LANES:]),
            ([s2, in_2], c2[:, -LANES:]),
        ],
    )
    ways = (SWAP_X, SWAP_Y, SWAP_Z, MIDDLE)
    sums = at_once(*zip(ways, sums))
    pooled = normed_sum(added(sum_own, *sums))
    rx_b0, ry_b0, rz_b0, over_2 = at_once(*zip(ways, (sx0, sy0, s1, m2)))
    return added(g1[0], rx_b0, ry_b0, rz_b0, over_2), pooled


def slot_table(chosen_ids, expert_count):
    chosen = (
        chosen_ids[:, :, None] == jnp.arange(expert_count, dtype=jnp.int32)[None, None, :]
    ).astype(jnp.int32)
    per_token = jnp.sum(chosen, axis=1)
    before = jnp.cumsum(per_token, axis=0) - per_token
    return jnp.sum(chosen * before[:, None, :], axis=2)


def expert_ffn(rows_in, weights_gu, weights_down):
    model_width = rows_in.shape[-1]
    flat_rows = rows_in.reshape(-1, model_width)
    hidden_width = weights_down.shape[0]
    gate_and_up = jnp.dot(flat_rows, weights_gu, preferred_element_type=jnp.float32)
    hidden = (jax.nn.silu(gate_and_up[:, :hidden_width]) * gate_and_up[:, hidden_width:]).astype(
        jnp.bfloat16
    )
    result = jnp.dot(hidden, weights_down, preferred_element_type=jnp.float32).astype(jnp.bfloat16)
    return result.reshape(rows_in.shape)


def exchanged_layer(normed, expert_ids, gate_norm, weights_gu, weights_down, capacity):
    tok_count, top_count = expert_ids.shape
    model_width = normed.shape[1]
    expert_count = lax.axis_size("center") * lax.axis_size("expert")
    position = slot_table(expert_ids, expert_count)
    target = (expert_ids * capacity + position).reshape(-1)
    repeated = jnp.broadcast_to(normed[:, None, :], (tok_count, top_count, model_width)).reshape(
        -1, model_width
    )
    send_buffer = (
        jnp.zeros((expert_count * capacity, model_width), jnp.bfloat16).at[target].set(repeated)
    )
    send_buffer = send_buffer.reshape(expert_count, capacity, model_width)
    computed = expert_ffn(
        lax.all_to_all(send_buffer, BOTH, split_axis=0, concat_axis=0, tiled=True),
        weights_gu,
        weights_down,
    )
    returned = lax.all_to_all(computed, BOTH, split_axis=0, concat_axis=0, tiled=True)
    returned = returned.reshape(expert_count * capacity, model_width)
    gathered = returned[target].reshape(tok_count, top_count, model_width)
    return jnp.sum(gathered.astype(jnp.float32) * gate_norm[:, :, None], axis=1)


def local(tokens, doc_ids, expert_ids, gate_raw, gate_up, down, bank):
    center_count = lax.axis_size("center")
    expert_axis = lax.axis_size("expert")
    expert_count = center_count * expert_axis
    tok_count, top_count = expert_ids.shape
    capacity = min(tok_count, 2 * tok_count * top_count // expert_count)
    weights_gu = gate_up[0]
    weights_down = down[0]
    bank_values = bank.astype(jnp.float32)
    bank_norms = jnp.sum(bank_values * bank_values, axis=1)
    if center_count == 8 and expert_axis == 4:
        rows = enter(tokens, expert_ids, gate_raw, doc_ids, expert_count)
        center_at, expert_at = lax.axis_index("center"), lax.axis_index("expert")
        who = jnp.stack(
            [center_at * expert_axis + expert_at, (center_at ^ CORE) * expert_axis + expert_at]
        ).astype(jnp.int32)
        combined, pooled = gathered_layer(
            rows, who, weights_gu, weights_down, capacity, expert_count, bank_norms
        )
    else:
        gate_norm = gate_raw / jnp.sum(gate_raw, axis=1, keepdims=True)
        combined = exchanged_layer(
            rms_normed(tokens), expert_ids, gate_norm, weights_gu, weights_down, capacity
        )
        member = (jnp.arange(DOC_DEV, dtype=jnp.int32)[:, None] == doc_ids[0][None, :]).astype(
            jnp.float32
        )
        summed = jnp.dot(
            member, combined, precision=lax.Precision.HIGHEST, preferred_element_type=jnp.float32
        )
        pooled = normed_sum(summed)
    layer_out = combined.astype(jnp.bfloat16)
    shard_part = lax.all_gather(pooled, "center", axis=0, tiled=True)
    doc_values = shard_part.astype(jnp.float32)
    doc_norms = jnp.sum(doc_values * doc_values, axis=1)
    products = lax.dot_general(
        shard_part, bank, (((1,), (1,)), ((), ())), preferred_element_type=jnp.float32
    )
    distance = doc_norms[:, None] + bank_norms[None, :] - 2.0 * products
    nearest = jnp.min(distance, axis=1)
    if center_count == 8 and expert_axis == 4:
        ways = (SWAP_X, SWAP_Y, SWAP_XY)
        for arrived in at_once(*[(way, nearest) for way in ways], behind=(layer_out,)):
            nearest = jnp.minimum(nearest, arrived)
        nearest = jnp.minimum(nearest, at_once((SWAP_CORE, nearest))[0])
    else:
        nearest = lax.pmin(nearest, "center")
    own_scores = lax.dynamic_slice_in_dim(nearest, lax.axis_index("center") * DOC_DEV, DOC_DEV)
    return (layer_out, own_scores)


def solution(mesh):
    return jax.shard_map(
        local,
        mesh=mesh,
        in_specs=(
            P(BOTH, None),
            P(BOTH, None),
            P(BOTH, None),
            P(BOTH, None),
            P(BOTH, None, None),
            P(BOTH, None, None),
            P("center", None),
        ),
        out_specs=(P(BOTH, None), P(BOTH)),
        check_vma=False,
    )
```

```python
import functools

import jax
import jax.numpy as jnp
from jax import lax
from jax.experimental import pallas as pl
from jax.experimental.pallas import tpu as pltpu
from jax.sharding import PartitionSpec as P

DOC_DEV = 8
BOTH = ("center", "expert")
CORE, ALONG_X, ALONG_Y = 1, 2, 4
LANES = 128


def rms_normed(hidden_rows):
    values = hidden_rows.astype(jnp.float32)
    inverse_rms = lax.rsqrt(jnp.mean(values * values, axis=-1, keepdims=True) + 1e-06)
    return (values * inverse_rms).astype(jnp.bfloat16)


KERNEL = pltpu.CompilerParams(vmem_limit_bytes=24 * 1024 * 1024)
ANYWHERE = pl.BlockSpec(memory_space=pltpu.HBM)
IN_VMEM = pl.BlockSpec(memory_space=pltpu.VMEM)
BESIDE = pl.CostEstimate(flops=1000, bytes_accessed=1000, transcendentals=0)
IN_SMEM = pl.BlockSpec(memory_space=pltpu.SMEM)
BF16 = jnp.bfloat16


def gate_lanes(shape, expert, expert_count):
    lane = lax.broadcasted_iota(jnp.int32, shape, len(shape) - 1)
    return (
        (lane == expert) | (lane == expert + expert_count) | (lane == expert + 2 * expert_count)
    )


def pick_kernel(capacity, expert_count, who_ref, *refs):
    count = len(refs) - 3
    blocks = refs[:count]
    mine, other, choice = refs[count:]
    tok_count = blocks[0].shape[0]
    model_width = blocks[0].shape[1] - LANES
    row = lax.broadcasted_iota(jnp.int32, (8, LANES), 0)
    asked = jnp.where(
        row == 0,
        gate_lanes((8, LANES), who_ref[0], expert_count).astype(jnp.float32),
        gate_lanes((8, LANES), who_ref[1], expert_count).astype(jnp.float32),
    ).astype(BF16)
    before = (
        lax.broadcasted_iota(jnp.int32, (tok_count, tok_count), 0)
        < lax.broadcasted_iota(jnp.int32, (tok_count, tok_count), 1)
    ).astype(jnp.float32).astype(BF16)
    slot_row = lax.broadcasted_iota(jnp.int32, (2 * capacity, tok_count), 0)
    first_half = slot_row < capacity
    slot_row = slot_row.astype(jnp.float32)
    tails = jnp.concatenate([block[:, pl.ds(model_width, LANES)] for block in blocks], axis=0)
    gates = lax.dot_general(
        asked, tails, (((1,), (1,)), ((), ())), preferred_element_type=jnp.float32
    )
    named = gates != 0.0
    ones = named.astype(jnp.float32).astype(BF16)
    for j in range(count):
        at = j * tok_count
        slot = jnp.dot(ones[:, at : at + tok_count], before, preferred_element_type=jnp.float32)
        slot = jnp.where(named[:, at : at + tok_count], slot, -1.0 - 2.0 * capacity)
        slot = jnp.where(first_half, slot[0:1, :], slot[1:2, :] + float(capacity))
        choice[j] = (slot == slot_row).astype(jnp.float32).astype(BF16)
    for j in range(count):
        picked = jnp.dot(choice[j], blocks[j][...], preferred_element_type=jnp.float32).astype(BF16)
        here = pl.ds(j * capacity, capacity)
        mine[here, :] = picked[:capacity]
        other[here, :] = picked[capacity:]


def pick(capacity, expert_count, who, blocks):
    count, tok_count, row_width = len(blocks), *blocks[0].shape
    picked = (count * capacity, row_width)
    choice = (count, 2 * capacity, tok_count)
    return pl.pallas_call(
        functools.partial(pick_kernel, capacity, expert_count),
        out_shape=[jax.ShapeDtypeStruct(shape, BF16) for shape in (picked, picked, choice)],
        in_specs=[IN_SMEM] + [IN_VMEM] * count,
        out_specs=[IN_VMEM] * 3,
        compiler_params=KERNEL,
        cost_estimate=BESIDE,
        name="pick",
    )(who, *blocks)


def expert_kernel(expert_count, count, who_ref, *refs):
    parts = refs[:count]
    gate_up, down = refs[count : count + 2]
    outs = refs[count + 2 : 2 * count + 2]
    hidden = refs[2 * count + 2]
    row_count = hidden.shape[0]
    hidden_width, model_width = down.shape
    tile = 256
    hidden_tiles, model_tiles = hidden_width // tile, model_width // tile
    starts = [0]
    for part in parts:
        starts.append(starts[-1] + part.shape[0])

    def columns(at, size):
        return jnp.concatenate([part[:, pl.ds(at, size)] for part in parts], axis=0)

    tail = columns(model_width, LANES).astype(jnp.float32)
    gate_column = jnp.sum(
        jnp.where(gate_lanes((row_count, LANES), who_ref[0], expert_count), tail, 0.0),
        axis=1,
        keepdims=True,
    )
    for step in range(hidden_tiles):
        at = step * tile
        values = columns(0, model_width)
        gate = jnp.dot(values, gate_up[:, pl.ds(at, tile)], preferred_element_type=jnp.float32)
        up = jnp.dot(
            values,
            gate_up[:, pl.ds(at + hidden_width, tile)],
            preferred_element_type=jnp.float32,
        )
        hidden[:, pl.ds(at, tile)] = (gate / (1.0 + jnp.exp(-gate)) * up).astype(BF16)
    for step in range(model_tiles):
        at = step * tile
        product = jnp.dot(
            hidden[...], down[:, pl.ds(at, tile)], preferred_element_type=jnp.float32
        )
        product = (product * gate_column).astype(BF16)
        for i, out in enumerate(outs):
            out[:, pl.ds(at, tile)] = product[starts[i] : starts[i + 1]]


def expert_rows(expert_count, who, parts, weights_gu, weights_down):
    hidden_width, model_width = weights_down.shape
    rows = sum(part.shape[0] for part in parts)
    outs = [jax.ShapeDtypeStruct((part.shape[0], model_width), BF16) for part in parts]
    return pl.pallas_call(
        functools.partial(expert_kernel, expert_count, len(parts)),
        out_shape=outs,
        in_specs=[IN_SMEM] + [IN_VMEM] * (len(parts) + 2),
        out_specs=[IN_VMEM] * len(parts),
        scratch_shapes=[pltpu.VMEM((rows, hidden_width), BF16)],
        compiler_params=KERNEL,
        cost_estimate=BESIDE,
        name="expert_rows",
    )(who, *parts, weights_gu, weights_down)


def put_kernel(choice, mine, other, *outs):
    capacity = choice.shape[1] // 2
    for j, out in enumerate(outs):
        here = pl.ds(j * capacity, capacity)
        rows = jnp.concatenate([mine[here, :], other[here, :]], axis=0)
        out[...] = lax.dot_general(
            choice[j], rows, (((0,), (0,)), ((), ())), preferred_element_type=jnp.float32
        ).astype(BF16)


def put(choice, mine, other):
    count, _, tok_count = choice.shape
    model_width = mine.shape[1]
    return pl.pallas_call(
        put_kernel,
        out_shape=[jax.ShapeDtypeStruct((tok_count, model_width), BF16)] * count,
        in_specs=[IN_VMEM] * 3,
        out_specs=[IN_VMEM] * count,
        compiler_params=KERNEL,
        cost_estimate=BESIDE,
        name="put",
    )(choice, mine, other)


def normed_sum(summed):
    return (summed * lax.rsqrt(jnp.sum(summed * summed, axis=1, keepdims=True) + 1e-06)).astype(
        jnp.bfloat16
    )


def added(*terms):
    total = terms[0].astype(jnp.float32)
    for term in terms[1:]:
        total = total + term.astype(jnp.float32)
    return total


def enter_kernel(expert_count, *refs):
    sources, rows_ref, targets, sem = refs[:4], refs[4], refs[5:9], refs[9]
    copies = [
        pltpu.make_async_copy(source, target, sem.at[i])
        for i, (source, target) in enumerate(zip(sources, targets))
    ]
    for copy in copies:
        copy.start()
    tokens_ref, ids_ref, gates_ref, docs_ref = targets
    tok_count, model_width = tokens_ref.shape
    for copy in copies[1:]:
        copy.wait()
    raw = gates_ref[...]
    gates = raw / jnp.sum(raw, axis=0, keepdims=True)
    ids = ids_ref[...]
    lane = lax.broadcasted_iota(jnp.int32, (LANES, tok_count), 0)
    table = jnp.zeros((LANES, tok_count), jnp.float32)
    for term in range(3):
        for choice in range(ids.shape[0]):
            hit = lane == ids[choice : choice + 1, :] + term * expert_count
            table = jnp.where(hit, gates[choice : choice + 1, :], table)
    first = table.astype(BF16).astype(jnp.float32)
    rest = table - first
    second = rest.astype(BF16).astype(jnp.float32)
    table = jnp.where(
        lane < expert_count, first, jnp.where(lane < 2 * expert_count, second, rest - second)
    )
    table = jnp.where(lane == 3 * expert_count, docs_ref[...].astype(jnp.float32), table)
    rows_ref[:, pl.ds(model_width, LANES)] = jnp.transpose(table).astype(BF16)
    copies[0].wait()
    rows_ref[:, pl.ds(0, model_width)] = rms_normed(tokens_ref[...])


def enter(tokens, expert_ids, gate_raw, doc_ids, expert_count):
    tok_count, model_width = tokens.shape
    return pl.pallas_call(
        functools.partial(enter_kernel, expert_count),
        out_shape=jax.ShapeDtypeStruct((tok_count, model_width + LANES), BF16),
        in_specs=[ANYWHERE] * 4,
        out_specs=IN_VMEM,
        scratch_shapes=[
            pltpu.VMEM(operand.shape, operand.dtype)
            for operand in (tokens, expert_ids.T, gate_raw.T, doc_ids)
        ]
        + [pltpu.SemaphoreType.DMA((4,))],
        compiler_params=pltpu.CompilerParams(vmem_limit_bytes=62 * 1024 * 1024),
        cost_estimate=BESIDE,
        name="enter",
    )(tokens, expert_ids.T, gate_raw.T, doc_ids)


def leave_kernel(doc_lane, sizes, *refs):
    refs = list(refs)
    groups, tails = [], []
    for size in sizes:
        groups.append([refs.pop(0) for _ in range(size)])
        tails.append(refs.pop(0))
    blocks, sums = refs[: len(sizes) - 1], refs[len(sizes) - 1 :]
    for i, group in enumerate(groups):
        total = group[0][...]
        if len(group) > 1:
            total = added(*[term[...] for term in group]).astype(BF16)
            blocks[i - 1][...] = total
        lane = lax.broadcasted_iota(jnp.int32, tails[i].shape, 1)
        named = tails[i][...].astype(jnp.float32)
        named = jnp.sum(jnp.where(lane == doc_lane, named, 0.0), axis=1, keepdims=True)
        member = (named == lane.astype(jnp.float32)).astype(jnp.float32).astype(BF16)
        sums[i][...] = lax.dot_general(
            member, total, (((0,), (0,)), ((), ())), preferred_element_type=jnp.float32
        )[:DOC_DEV]


def leave(doc_lane, groups):
    tok_count, model_width = groups[0][0][0].shape
    operands = [ref for blocks, tail in groups for ref in (*blocks, tail)]
    count = len(groups)
    results = pl.pallas_call(
        functools.partial(leave_kernel, doc_lane, [len(blocks) for blocks, _ in groups]),
        out_shape=[jax.ShapeDtypeStruct((tok_count, model_width), BF16)] * (count - 1)
        + [jax.ShapeDtypeStruct((DOC_DEV, model_width), jnp.float32)] * count,
        in_specs=[IN_VMEM] * len(operands),
        out_specs=[IN_VMEM] * (2 * count - 1),
        compiler_params=KERNEL,
        cost_estimate=BESIDE,
        name="leave",
    )(*operands)
    return results[: count - 1], results[count - 1 :]


SWAP_X = ("center", tuple((i, i ^ ALONG_X) for i in range(8)))
SWAP_Y = ("center", tuple((i, i ^ ALONG_Y) for i in range(8)))
SWAP_XY = ("center", tuple((i, i ^ ALONG_X ^ ALONG_Y) for i in range(8)))
SWAP_CORE = ("center", tuple((i, i ^ CORE) for i in range(8)))
SWAP_Z = ("expert", ((0, 1), (1, 0), (2, 3), (3, 2)))
MIDDLE = ("expert", ((1, 2), (2, 1)))


def at_once(*sends, behind=()):
    values = [value for _, value in sends]
    if len(behind) > 0:
        held = lax.optimization_barrier((tuple(values), tuple(behind)))
        values = held[0]
    return [lax.ppermute(value, way[0], way[1]) for (way, _), value in zip(sends, values)]


def gathered_layer(rows, who, weights_gu, weights_down, capacity, expert_count, beside):
    def picked(*blocks):
        return pick(capacity, expert_count, who, blocks)

    def crossed(values):
        return at_once((SWAP_CORE, values))[0]

    def results(*parts):
        return expert_rows(expert_count, who, parts, weights_gu, weights_down)

    def worked(*groups):
        parts = [part for mine, other, _ in groups for part in (mine, other)]
        done = results(*parts)
        return [(groups[i][2], done[2 * i], done[2 * i + 1]) for i in range(len(groups))]

    b0 = rows
    bx0, by0, b1, c2 = at_once((SWAP_X, b0), (SWAP_Y, b0), (SWAP_Z, b0), (MIDDLE, b0))
    d0, by1, o2, c3 = at_once(
        (SWAP_X, by0), (SWAP_Y, b1), (SWAP_Z, c2), (MIDDLE, b1),
        behind=(bx0, by0, b1, c2),
    )
    mine, other, choice = picked(b0, bx0, by0, b1)
    first = (mine, crossed(other), choice)
    b2 = c2 + o2
    bx2, by2, o3 = at_once(
        (SWAP_X, b2), (SWAP_Y, b2), (SWAP_Z, c3), behind=(d0, by1, c3, mine, beside)
    )
    mine, other, choice = picked(d0, by1, b2)
    second = (mine, crossed(other), choice)
    b3 = c3 + o3
    bx3, by3, bx1 = at_once(
        (SWAP_X, b3), (SWAP_Y, b3), (SWAP_Z, bx0), behind=(bx2, by2, mine)
    )
    mine, other, choice = picked(bx2, by2, b3)
    third = (mine, crossed(other), choice)
    (first,) = worked(first)
    d2, d3, d1 = at_once(
        (SWAP_X, by2), (SWAP_Y, bx3), (SWAP_Z, d0), behind=(bx3, by3, bx1, mine, first[1])
    )
    mine, other, choice = picked(bx3, by3, bx1)
    fourth = (mine, crossed(other), choice)
    (third,) = worked(third)
    (fourth_mine,) = results(lax.optimization_barrier((fourth[0], third[1]))[0])
    held = lax.optimization_barrier((d1, d2, d3, mine, third[1], fourth_mine))
    mine, other, choice = picked(*held[:3])
    last_mine, last_other = results(mine)[0], crossed(other)
    (last_other,) = results(lax.optimization_barrier((last_other, last_mine))[0])
    (fourth_other,) = results(lax.optimization_barrier((fourth[1], last_other))[0])
    g5 = put(choice, last_mine, crossed(last_other))
    rx_y2, ry_x3, rz_d0 = at_once((SWAP_X, g5[1]), (SWAP_Y, g5[2]), (SWAP_Z, g5[0]))
    fourth_other = crossed(fourth_other)
    g3 = put(*lax.optimization_barrier((third[0], third[1], crossed(third[2]), g5[0]))[:3])
    g4 = put(*lax.optimization_barrier((fourth[2], fourth_mine, fourth_other, g5[0]))[:3])
    second = (lax.optimization_barrier((second[0], g5[0]))[0], *second[1:])
    (second,) = worked(second)
    g2 = put(second[0], second[1], crossed(second[2]))
    g1 = put(*lax.optimization_barrier((first[0], first[1], crossed(first[2]), g4[0]))[:3])
    sx3 = added(g4[0], ry_x3).astype(BF16)
    rx_b3, ry_b3, rz_x0 = at_once(
        (SWAP_X, sx3), (SWAP_Y, g4[1]), (SWAP_Z, g4[2]), behind=(rx_y2, rz_d0, g4[0], second[1], g1[0], g3[0])
    )
    sy2 = added(g3[1], rx_y2).astype(BF16)
    s3 = added(g3[2], rx_b3, ry_b3).astype(BF16)
    rx_b2, ry_b2, in_3 = at_once(
        (SWAP_X, g3[0]), (SWAP_Y, sy2), (SWAP_Z, s3), behind=(rz_x0, g2[0])
    )
    sd0 = added(g2[0], rz_d0).astype(BF16)
    s2 = added(g2[2], rx_b2, ry_b2).astype(BF16)
    rx_y0, ry_b1, in_2, over_3 = at_once(
        (SWAP_X, sd0), (SWAP_Y, g2[1]), (SWAP_Z, s2),
        (MIDDLE, added(s3, in_3).astype(BF16)), behind=(rx_b2, ry_b2),
    )
    (sx0, sy0, s1, m2), (sum_own, *sums) = leave(
        3 * expert_count,
        [
            ([g1[0]], rows[:, -LANES:]),
            ([g1[1], rz_x0], bx0[:, -LANES:]),
            ([g1[2], rx_y0], by0[:, -LANES:]),
            ([g1[3], ry_b1, over_3], b1[:, -LANES:]),
            ([s2, in_2], c2[:, -LANES:]),
        ],
    )
    ways = (SWAP_X, SWAP_Y, SWAP_Z, MIDDLE)
    sums = at_once(*zip(ways, sums))
    pooled = normed_sum(added(sum_own, *sums))
    rx_b0, ry_b0, rz_b0, over_2 = at_once(*zip(ways, (sx0, sy0, s1, m2)))
    return added(g1[0], rx_b0, ry_b0, rz_b0, over_2), pooled


def slot_table(chosen_ids, expert_count):
    chosen = (
        chosen_ids[:, :, None] == jnp.arange(expert_count, dtype=jnp.int32)[None, None, :]
    ).astype(jnp.int32)
    per_token = jnp.sum(chosen, axis=1)
    before = jnp.cumsum(per_token, axis=0) - per_token
    return jnp.sum(chosen * before[:, None, :], axis=2)


def expert_ffn(rows_in, weights_gu, weights_down):
    model_width = rows_in.shape[-1]
    flat_rows = rows_in.reshape(-1, model_width)
    hidden_width = weights_down.shape[0]
    gate_and_up = jnp.dot(flat_rows, weights_gu, preferred_element_type=jnp.float32)
    hidden = (jax.nn.silu(gate_and_up[:, :hidden_width]) * gate_and_up[:, hidden_width:]).astype(
        jnp.bfloat16
    )
    result = jnp.dot(hidden, weights_down, preferred_element_type=jnp.float32).astype(jnp.bfloat16)
    return result.reshape(rows_in.shape)


def exchanged_layer(normed, expert_ids, gate_norm, weights_gu, weights_down, capacity):
    tok_count, top_count = expert_ids.shape
    model_width = normed.shape[1]
    expert_count = lax.axis_size("center") * lax.axis_size("expert")
    position = slot_table(expert_ids, expert_count)
    target = (expert_ids * capacity + position).reshape(-1)
    repeated = jnp.broadcast_to(normed[:, None, :], (tok_count, top_count, model_width)).reshape(
        -1, model_width
    )
    send_buffer = (
        jnp.zeros((expert_count * capacity, model_width), jnp.bfloat16).at[target].set(repeated)
    )
    send_buffer = send_buffer.reshape(expert_count, capacity, model_width)
    computed = expert_ffn(
        lax.all_to_all(send_buffer, BOTH, split_axis=0, concat_axis=0, tiled=True),
        weights_gu,
        weights_down,
    )
    returned = lax.all_to_all(computed, BOTH, split_axis=0, concat_axis=0, tiled=True)
    returned = returned.reshape(expert_count * capacity, model_width)
    gathered = returned[target].reshape(tok_count, top_count, model_width)
    return jnp.sum(gathered.astype(jnp.float32) * gate_norm[:, :, None], axis=1)


def local(tokens, doc_ids, expert_ids, gate_raw, gate_up, down, bank):
    center_count = lax.axis_size("center")
    expert_axis = lax.axis_size("expert")
    expert_count = center_count * expert_axis
    tok_count, top_count = expert_ids.shape
    capacity = min(tok_count, 2 * tok_count * top_count // expert_count)
    weights_gu = gate_up[0]
    weights_down = down[0]
    bank_values = bank.astype(jnp.float32)
    bank_norms = jnp.sum(bank_values * bank_values, axis=1)
    if center_count == 8 and expert_axis == 4:
        rows = enter(tokens, expert_ids, gate_raw, doc_ids, expert_count)
        center_at, expert_at = lax.axis_index("center"), lax.axis_index("expert")
        who = jnp.stack(
            [center_at * expert_axis + expert_at, (center_at ^ CORE) * expert_axis + expert_at]
        ).astype(jnp.int32)
        combined, pooled = gathered_layer(
            rows, who, weights_gu, weights_down, capacity, expert_count, bank_norms
        )
    else:
        gate_norm = gate_raw / jnp.sum(gate_raw, axis=1, keepdims=True)
        combined = exchanged_layer(
            rms_normed(tokens), expert_ids, gate_norm, weights_gu, weights_down, capacity
        )
        member = (jnp.arange(DOC_DEV, dtype=jnp.int32)[:, None] == doc_ids[0][None, :]).astype(
            jnp.float32
        )
        summed = jnp.dot(
            member, combined, precision=lax.Precision.HIGHEST, preferred_element_type=jnp.float32
        )
        pooled = normed_sum(summed)
    layer_out = combined.astype(jnp.bfloat16)
    shard_part = lax.all_gather(pooled, "center", axis=0, tiled=True)
    doc_values = shard_part.astype(jnp.float32)
    doc_norms = jnp.sum(doc_values * doc_values, axis=1)
    products = lax.dot_general(
        shard_part, bank, (((1,), (1,)), ((), ())), preferred_element_type=jnp.float32
    )
    distance = doc_norms[:, None] + bank_norms[None, :] - 2.0 * products
    nearest = jnp.min(distance, axis=1)
    if center_count == 8 and expert_axis == 4:
        ways = (SWAP_X, SWAP_Y, SWAP_XY)
        for arrived in at_once(*[(way, nearest) for way in ways], behind=(layer_out,)):
            nearest = jnp.minimum(nearest, arrived)
        nearest = jnp.minimum(nearest, at_once((SWAP_CORE, nearest))[0])
    else:
        nearest = lax.pmin(nearest, "center")
    own_scores = lax.dynamic_slice_in_dim(nearest, lax.axis_index("center") * DOC_DEV, DOC_DEV)
    return (layer_out, own_scores)


def solution(mesh):
    return jax.shard_map(
        local,
        mesh=mesh,
        in_specs=(
            P(BOTH, None),
            P(BOTH, None),
            P(BOTH, None),
            P(BOTH, None),
            P(BOTH, None, None),
            P(BOTH, None, None),
            P("center", None),
        ),
        out_specs=(P(BOTH, None), P(BOTH)),
        check_vma=False,
    )
```

```python
import functools

import jax
import jax.numpy as jnp
from jax import lax
from jax.experimental import pallas as pl
from jax.experimental.pallas import tpu as pltpu
from jax.sharding import PartitionSpec as P

DOC_DEV = 8
BOTH = ("center", "expert")
CORE, ALONG_X, ALONG_Y = 1, 2, 4
LANES = 128


def rms_normed(hidden_rows):
    values = hidden_rows.astype(jnp.float32)
    inverse_rms = lax.rsqrt(jnp.mean(values * values, axis=-1, keepdims=True) + 1e-06)
    return (values * inverse_rms).astype(jnp.bfloat16)


KERNEL = pltpu.CompilerParams(vmem_limit_bytes=24 * 1024 * 1024)
ANYWHERE = pl.BlockSpec(memory_space=pltpu.HBM)
IN_VMEM = pl.BlockSpec(memory_space=pltpu.VMEM)
BESIDE = pl.CostEstimate(flops=1000, bytes_accessed=1000, transcendentals=0)
IN_SMEM = pl.BlockSpec(memory_space=pltpu.SMEM)
BF16 = jnp.bfloat16


def gate_lanes(shape, expert, expert_count):
    lane = lax.broadcasted_iota(jnp.int32, shape, len(shape) - 1)
    return (
        (lane == expert) | (lane == expert + expert_count) | (lane == expert + 2 * expert_count)
    )


def pick_kernel(capacity, expert_count, who_ref, *refs):
    count = len(refs) - 3
    blocks = refs[:count]
    mine, other, choice = refs[count:]
    tok_count = blocks[0].shape[0]
    model_width = blocks[0].shape[1] - LANES
    row = lax.broadcasted_iota(jnp.int32, (8, LANES), 0)
    asked = jnp.where(
        row == 0,
        gate_lanes((8, LANES), who_ref[0], expert_count).astype(jnp.float32),
        gate_lanes((8, LANES), who_ref[1], expert_count).astype(jnp.float32),
    ).astype(BF16)
    before = (
        lax.broadcasted_iota(jnp.int32, (tok_count, tok_count), 0)
        < lax.broadcasted_iota(jnp.int32, (tok_count, tok_count), 1)
    ).astype(jnp.float32).astype(BF16)
    slot_row = lax.broadcasted_iota(jnp.int32, (2 * capacity, tok_count), 0)
    first_half = slot_row < capacity
    slot_row = slot_row.astype(jnp.float32)
    tails = jnp.concatenate([block[:, pl.ds(model_width, LANES)] for block in blocks], axis=0)
    gates = lax.dot_general(
        asked, tails, (((1,), (1,)), ((), ())), preferred_element_type=jnp.float32
    )
    named = gates != 0.0
    ones = named.astype(jnp.float32).astype(BF16)
    for j in range(count):
        at = j * tok_count
        slot = jnp.dot(ones[:, at : at + tok_count], before, preferred_element_type=jnp.float32)
        slot = jnp.where(named[:, at : at + tok_count], slot, -1.0 - 2.0 * capacity)
        slot = jnp.where(first_half, slot[0:1, :], slot[1:2, :] + float(capacity))
        choice[j] = (slot == slot_row).astype(jnp.float32).astype(BF16)
    for j in range(count):
        picked = jnp.dot(choice[j], blocks[j][...], preferred_element_type=jnp.float32).astype(BF16)
        here = pl.ds(j * capacity, capacity)
        mine[here, :] = picked[:capacity]
        other[here, :] = picked[capacity:]


def pick(capacity, expert_count, who, blocks):
    count, tok_count, row_width = len(blocks), *blocks[0].shape
    picked = (count * capacity, row_width)
    choice = (count, 2 * capacity, tok_count)
    return pl.pallas_call(
        functools.partial(pick_kernel, capacity, expert_count),
        out_shape=[jax.ShapeDtypeStruct(shape, BF16) for shape in (picked, picked, choice)],
        in_specs=[IN_SMEM] + [IN_VMEM] * count,
        out_specs=[IN_VMEM] * 3,
        compiler_params=KERNEL,
        cost_estimate=BESIDE,
        name="pick",
    )(who, *blocks)


def expert_kernel(expert_count, count, who_ref, *refs):
    parts = refs[:count]
    gate_up, down = refs[count : count + 2]
    outs = refs[count + 2 : 2 * count + 2]
    hidden = refs[2 * count + 2]
    row_count = hidden.shape[0]
    hidden_width, model_width = down.shape
    tile = 256
    hidden_tiles, model_tiles = hidden_width // tile, model_width // tile
    starts = [0]
    for part in parts:
        starts.append(starts[-1] + part.shape[0])

    def columns(at, size):
        return jnp.concatenate([part[:, pl.ds(at, size)] for part in parts], axis=0)

    tail = columns(model_width, LANES).astype(jnp.float32)
    gate_column = jnp.sum(
        jnp.where(gate_lanes((row_count, LANES), who_ref[0], expert_count), tail, 0.0),
        axis=1,
        keepdims=True,
    )
    for step in range(hidden_tiles):
        at = step * tile
        values = columns(0, model_width)
        gate = jnp.dot(values, gate_up[:, pl.ds(at, tile)], preferred_element_type=jnp.float32)
        up = jnp.dot(
            values,
            gate_up[:, pl.ds(at + hidden_width, tile)],
            preferred_element_type=jnp.float32,
        )
        hidden[:, pl.ds(at, tile)] = (gate / (1.0 + jnp.exp(-gate)) * up).astype(BF16)
    for step in range(model_tiles):
        at = step * tile
        product = jnp.dot(
            hidden[...], down[:, pl.ds(at, tile)], preferred_element_type=jnp.float32
        )
        product = (product * gate_column).astype(BF16)
        for i, out in enumerate(outs):
            out[:, pl.ds(at, tile)] = product[starts[i] : starts[i + 1]]


def expert_rows(expert_count, who, parts, weights_gu, weights_down):
    hidden_width, model_width = weights_down.shape
    rows = sum(part.shape[0] for part in parts)
    outs = [jax.ShapeDtypeStruct((part.shape[0], model_width), BF16) for part in parts]
    return pl.pallas_call(
        functools.partial(expert_kernel, expert_count, len(parts)),
        out_shape=outs,
        in_specs=[IN_SMEM] + [IN_VMEM] * (len(parts) + 2),
        out_specs=[IN_VMEM] * len(parts),
        scratch_shapes=[pltpu.VMEM((rows, hidden_width), BF16)],
        compiler_params=KERNEL,
        cost_estimate=BESIDE,
        name="expert_rows",
    )(who, *parts, weights_gu, weights_down)


def put_kernel(choice, mine, other, *outs):
    capacity = choice.shape[1] // 2
    for j, out in enumerate(outs):
        here = pl.ds(j * capacity, capacity)
        rows = jnp.concatenate([mine[here, :], other[here, :]], axis=0)
        out[...] = lax.dot_general(
            choice[j], rows, (((0,), (0,)), ((), ())), preferred_element_type=jnp.float32
        ).astype(BF16)


def put(choice, mine, other):
    count, _, tok_count = choice.shape
    model_width = mine.shape[1]
    return pl.pallas_call(
        put_kernel,
        out_shape=[jax.ShapeDtypeStruct((tok_count, model_width), BF16)] * count,
        in_specs=[IN_VMEM] * 3,
        out_specs=[IN_VMEM] * count,
        compiler_params=KERNEL,
        cost_estimate=BESIDE,
        name="put",
    )(choice, mine, other)


def normed_sum(summed):
    return (summed * lax.rsqrt(jnp.sum(summed * summed, axis=1, keepdims=True) + 1e-06)).astype(
        jnp.bfloat16
    )


def added(*terms):
    total = terms[0].astype(jnp.float32)
    for term in terms[1:]:
        total = total + term.astype(jnp.float32)
    return total


def enter_kernel(expert_count, *refs):
    sources, rows_ref, targets, sem = refs[:4], refs[4], refs[5:9], refs[9]
    copies = [
        pltpu.make_async_copy(source, target, sem.at[i])
        for i, (source, target) in enumerate(zip(sources, targets))
    ]
    for copy in copies:
        copy.start()
    tokens_ref, ids_ref, gates_ref, docs_ref = targets
    tok_count, model_width = tokens_ref.shape
    for copy in copies[1:]:
        copy.wait()
    raw = gates_ref[...]
    gates = raw / jnp.sum(raw, axis=0, keepdims=True)
    ids = ids_ref[...]
    lane = lax.broadcasted_iota(jnp.int32, (LANES, tok_count), 0)
    table = jnp.zeros((LANES, tok_count), jnp.float32)
    for term in range(3):
        for choice in range(ids.shape[0]):
            hit = lane == ids[choice : choice + 1, :] + term * expert_count
            table = jnp.where(hit, gates[choice : choice + 1, :], table)
    first = table.astype(BF16).astype(jnp.float32)
    rest = table - first
    second = rest.astype(BF16).astype(jnp.float32)
    table = jnp.where(
        lane < expert_count, first, jnp.where(lane < 2 * expert_count, second, rest - second)
    )
    table = jnp.where(lane == 3 * expert_count, docs_ref[...].astype(jnp.float32), table)
    rows_ref[:, pl.ds(model_width, LANES)] = jnp.transpose(table).astype(BF16)
    copies[0].wait()
    rows_ref[:, pl.ds(0, model_width)] = rms_normed(tokens_ref[...])


def enter(tokens, expert_ids, gate_raw, doc_ids, expert_count):
    tok_count, model_width = tokens.shape
    return pl.pallas_call(
        functools.partial(enter_kernel, expert_count),
        out_shape=jax.ShapeDtypeStruct((tok_count, model_width + LANES), BF16),
        in_specs=[ANYWHERE] * 4,
        out_specs=IN_VMEM,
        scratch_shapes=[
            pltpu.VMEM(operand.shape, operand.dtype)
            for operand in (tokens, expert_ids.T, gate_raw.T, doc_ids)
        ]
        + [pltpu.SemaphoreType.DMA((4,))],
        compiler_params=pltpu.CompilerParams(vmem_limit_bytes=62 * 1024 * 1024),
        cost_estimate=BESIDE,
        name="enter",
    )(tokens, expert_ids.T, gate_raw.T, doc_ids)


def leave_kernel(doc_lane, sizes, *refs):
    refs = list(refs)
    groups, tails = [], []
    for size in sizes:
        groups.append([refs.pop(0) for _ in range(size)])
        tails.append(refs.pop(0))
    blocks, sums = refs[: len(sizes) - 1], refs[len(sizes) - 1 :]
    for i, group in enumerate(groups):
        total = group[0][...]
        if len(group) > 1:
            total = added(*[term[...] for term in group]).astype(BF16)
            blocks[i - 1][...] = total
        lane = lax.broadcasted_iota(jnp.int32, tails[i].shape, 1)
        named = tails[i][...].astype(jnp.float32)
        named = jnp.sum(jnp.where(lane == doc_lane, named, 0.0), axis=1, keepdims=True)
        member = (named == lane.astype(jnp.float32)).astype(jnp.float32).astype(BF16)
        sums[i][...] = lax.dot_general(
            member, total, (((0,), (0,)), ((), ())), preferred_element_type=jnp.float32
        )[:DOC_DEV]


def leave(doc_lane, groups):
    tok_count, model_width = groups[0][0][0].shape
    operands = [ref for blocks, tail in groups for ref in (*blocks, tail)]
    count = len(groups)
    results = pl.pallas_call(
        functools.partial(leave_kernel, doc_lane, [len(blocks) for blocks, _ in groups]),
        out_shape=[jax.ShapeDtypeStruct((tok_count, model_width), BF16)] * (count - 1)
        + [jax.ShapeDtypeStruct((DOC_DEV, model_width), jnp.float32)] * count,
        in_specs=[IN_VMEM] * len(operands),
        out_specs=[IN_VMEM] * (2 * count - 1),
        compiler_params=KERNEL,
        cost_estimate=BESIDE,
        name="leave",
    )(*operands)
    return results[: count - 1], results[count - 1 :]


SWAP_X = ("center", tuple((i, i ^ ALONG_X) for i in range(8)))
SWAP_Y = ("center", tuple((i, i ^ ALONG_Y) for i in range(8)))
SWAP_XY = ("center", tuple((i, i ^ ALONG_X ^ ALONG_Y) for i in range(8)))
SWAP_CORE = ("center", tuple((i, i ^ CORE) for i in range(8)))
SWAP_Z = ("expert", ((0, 1), (1, 0), (2, 3), (3, 2)))
MIDDLE = ("expert", ((1, 2), (2, 1)))


def at_once(*sends, behind=()):
    values = [value for _, value in sends]
    if len(behind) > 0:
        held = lax.optimization_barrier((tuple(values), tuple(behind)))
        values = held[0]
    return [lax.ppermute(value, way[0], way[1]) for (way, _), value in zip(sends, values)]


def gathered_layer(rows, who, weights_gu, weights_down, capacity, expert_count, beside):
    def picked(*blocks):
        return pick(capacity, expert_count, who, blocks)

    def crossed(values):
        return at_once((SWAP_CORE, values))[0]

    def results(*parts):
        return expert_rows(expert_count, who, parts, weights_gu, weights_down)

    def worked(*groups):
        parts = [part for mine, other, _ in groups for part in (mine, other)]
        done = results(*parts)
        return [(groups[i][2], done[2 * i], done[2 * i + 1]) for i in range(len(groups))]

    b0 = rows
    bx0, by0, b1, c2 = at_once((SWAP_X, b0), (SWAP_Y, b0), (SWAP_Z, b0), (MIDDLE, b0))
    d0, by1, o2, c3 = at_once(
        (SWAP_X, by0), (SWAP_Y, b1), (SWAP_Z, c2), (MIDDLE, b1),
        behind=(bx0, by0, b1, c2),
    )
    mine, other, choice = picked(b0, bx0, by0, b1)
    first = (mine, crossed(other), choice)
    b2 = c2 + o2
    bx2, by2, o3 = at_once(
        (SWAP_X, b2), (SWAP_Y, b2), (SWAP_Z, c3), behind=(d0, by1, c3, mine, beside)
    )
    mine, other, choice = picked(d0, by1, b2)
    second = (mine, crossed(other), choice)
    b3 = c3 + o3
    bx3, by3, bx1 = at_once(
        (SWAP_X, b3), (SWAP_Y, b3), (SWAP_Z, bx0), behind=(bx2, by2, mine)
    )
    mine, other, choice = picked(bx2, by2, b3)
    third = (mine, crossed(other), choice)
    (first,) = worked(first)
    d2, d3, d1 = at_once(
        (SWAP_X, by2), (SWAP_Y, bx3), (SWAP_Z, d0), behind=(bx3, by3, bx1, mine, first[1])
    )
    mine, other, choice = picked(bx3, by3, bx1)
    fourth = (mine, crossed(other), choice)
    (third,) = worked(third)
    (fourth_mine,) = results(lax.optimization_barrier((fourth[0], third[1]))[0])
    held = lax.optimization_barrier((d1, d2, d3, mine, third[1], fourth_mine))
    mine, other, choice = picked(*held[:3])
    last_mine, last_other = results(mine)[0], crossed(other)
    (last_other,) = results(lax.optimization_barrier((last_other, last_mine))[0])
    (fourth_other,) = results(lax.optimization_barrier((fourth[1], last_other))[0])
    g5 = put(choice, last_mine, crossed(last_other))
    rx_y2, ry_x3, rz_d0 = at_once((SWAP_X, g5[1]), (SWAP_Y, g5[2]), (SWAP_Z, g5[0]))
    fourth_other = crossed(fourth_other)
    g3 = put(*lax.optimization_barrier((third[0], third[1], crossed(third[2]), g5[0]))[:3])
    g4 = put(*lax.optimization_barrier((fourth[2], fourth_mine, fourth_other, g5[0]))[:3])
    second = (lax.optimization_barrier((second[0], g5[0]))[0], *second[1:])
    (second,) = worked(second)
    g2 = put(second[0], second[1], crossed(second[2]))
    g1 = put(*lax.optimization_barrier((first[0], first[1], crossed(first[2]), g4[0]))[:3])
    sx3 = added(g4[0], ry_x3).astype(BF16)
    rx_b3, ry_b3, rz_x0 = at_once(
        (SWAP_X, sx3), (SWAP_Y, g4[1]), (SWAP_Z, g4[2]), behind=(rx_y2, rz_d0, g4[0], second[1], g1[0], g3[0])
    )
    sy2 = added(g3[1], rx_y2).astype(BF16)
    s3 = added(g3[2], rx_b3, ry_b3).astype(BF16)
    rx_b2, ry_b2, in_3 = at_once(
        (SWAP_X, g3[0]), (SWAP_Y, sy2), (SWAP_Z, s3), behind=(rz_x0, g2[0])
    )
    (sx0,), (_, sum_x) = leave(
        3 * expert_count,
        [([g1[0]], rows[:, -LANES:]), ([g1[1], rz_x0], bx0[:, -LANES:])],
    )
    (sum_x,) = at_once((SWAP_X, sum_x), behind=(rx_b2,))
    sd0 = added(g2[0], rz_d0).astype(BF16)
    s2 = added(g2[2], rx_b2, ry_b2).astype(BF16)
    rx_y0, ry_b1, in_2, over_3 = at_once(
        (SWAP_X, sd0), (SWAP_Y, g2[1]), (SWAP_Z, s2),
        (MIDDLE, added(s3, in_3).astype(BF16)), behind=(rx_b2, ry_b2),
    )
    (sy0, s1, m2), (sum_own, *sums) = leave(
        3 * expert_count,
        [
            ([g1[0]], rows[:, -LANES:]),
            ([g1[2], rx_y0], by0[:, -LANES:]),
            ([g1[3], ry_b1, over_3], b1[:, -LANES:]),
            ([s2, in_2], c2[:, -LANES:]),
        ],
    )
    sums = at_once((SWAP_Y, sums[0]), (SWAP_Z, sums[1]), (MIDDLE, sums[2]))
    pooled = normed_sum(added(sum_own, sum_x, *sums))
    held = lax.optimization_barrier((sx0, rx_y0))[0]
    rx_b0, ry_b0, rz_b0, over_2 = at_once(
        (SWAP_X, held), (SWAP_Y, sy0), (SWAP_Z, s1), (MIDDLE, m2)
    )
    return added(g1[0], rx_b0, ry_b0, rz_b0, over_2), pooled


def slot_table(chosen_ids, expert_count):
    chosen = (
        chosen_ids[:, :, None] == jnp.arange(expert_count, dtype=jnp.int32)[None, None, :]
    ).astype(jnp.int32)
    per_token = jnp.sum(chosen, axis=1)
    before = jnp.cumsum(per_token, axis=0) - per_token
    return jnp.sum(chosen * before[:, None, :], axis=2)


def expert_ffn(rows_in, weights_gu, weights_down):
    model_width = rows_in.shape[-1]
    flat_rows = rows_in.reshape(-1, model_width)
    hidden_width = weights_down.shape[0]
    gate_and_up = jnp.dot(flat_rows, weights_gu, preferred_element_type=jnp.float32)
    hidden = (jax.nn.silu(gate_and_up[:, :hidden_width]) * gate_and_up[:, hidden_width:]).astype(
        jnp.bfloat16
    )
    result = jnp.dot(hidden, weights_down, preferred_element_type=jnp.float32).astype(jnp.bfloat16)
    return result.reshape(rows_in.shape)


def exchanged_layer(normed, expert_ids, gate_norm, weights_gu, weights_down, capacity):
    tok_count, top_count = expert_ids.shape
    model_width = normed.shape[1]
    expert_count = lax.axis_size("center") * lax.axis_size("expert")
    position = slot_table(expert_ids, expert_count)
    target = (expert_ids * capacity + position).reshape(-1)
    repeated = jnp.broadcast_to(normed[:, None, :], (tok_count, top_count, model_width)).reshape(
        -1, model_width
    )
    send_buffer = (
        jnp.zeros((expert_count * capacity, model_width), jnp.bfloat16).at[target].set(repeated)
    )
    send_buffer = send_buffer.reshape(expert_count, capacity, model_width)
    computed = expert_ffn(
        lax.all_to_all(send_buffer, BOTH, split_axis=0, concat_axis=0, tiled=True),
        weights_gu,
        weights_down,
    )
    returned = lax.all_to_all(computed, BOTH, split_axis=0, concat_axis=0, tiled=True)
    returned = returned.reshape(expert_count * capacity, model_width)
    gathered = returned[target].reshape(tok_count, top_count, model_width)
    return jnp.sum(gathered.astype(jnp.float32) * gate_norm[:, :, None], axis=1)


def local(tokens, doc_ids, expert_ids, gate_raw, gate_up, down, bank):
    center_count = lax.axis_size("center")
    expert_axis = lax.axis_size("expert")
    expert_count = center_count * expert_axis
    tok_count, top_count = expert_ids.shape
    capacity = min(tok_count, 2 * tok_count * top_count // expert_count)
    weights_gu = gate_up[0]
    weights_down = down[0]
    bank_values = bank.astype(jnp.float32)
    bank_norms = jnp.sum(bank_values * bank_values, axis=1)
    if center_count == 8 and expert_axis == 4:
        rows = enter(tokens, expert_ids, gate_raw, doc_ids, expert_count)
        center_at, expert_at = lax.axis_index("center"), lax.axis_index("expert")
        who = jnp.stack(
            [center_at * expert_axis + expert_at, (center_at ^ CORE) * expert_axis + expert_at]
        ).astype(jnp.int32)
        combined, pooled = gathered_layer(
            rows, who, weights_gu, weights_down, capacity, expert_count, bank_norms
        )
    else:
        gate_norm = gate_raw / jnp.sum(gate_raw, axis=1, keepdims=True)
        combined = exchanged_layer(
            rms_normed(tokens), expert_ids, gate_norm, weights_gu, weights_down, capacity
        )
        member = (jnp.arange(DOC_DEV, dtype=jnp.int32)[:, None] == doc_ids[0][None, :]).astype(
            jnp.float32
        )
        summed = jnp.dot(
            member, combined, precision=lax.Precision.HIGHEST, preferred_element_type=jnp.float32
        )
        pooled = normed_sum(summed)
    layer_out = combined.astype(jnp.bfloat16)
    shard_part = lax.all_gather(pooled, "center", axis=0, tiled=True)
    doc_values = shard_part.astype(jnp.float32)
    doc_norms = jnp.sum(doc_values * doc_values, axis=1)
    products = lax.dot_general(
        shard_part, bank, (((1,), (1,)), ((), ())), preferred_element_type=jnp.float32
    )
    distance = doc_norms[:, None] + bank_norms[None, :] - 2.0 * products
    nearest = jnp.min(distance, axis=1)
    if center_count == 8 and expert_axis == 4:
        ways = (SWAP_X, SWAP_Y, SWAP_XY)
        for arrived in at_once(*[(way, nearest) for way in ways], behind=(layer_out,)):
            nearest = jnp.minimum(nearest, arrived)
        nearest = jnp.minimum(nearest, at_once((SWAP_CORE, nearest))[0])
    else:
        nearest = lax.pmin(nearest, "center")
    own_scores = lax.dynamic_slice_in_dim(nearest, lax.axis_index("center") * DOC_DEV, DOC_DEV)
    return (layer_out, own_scores)


def solution(mesh):
    return jax.shard_map(
        local,
        mesh=mesh,
        in_specs=(
            P(BOTH, None),
            P(BOTH, None),
            P(BOTH, None),
            P(BOTH, None),
            P(BOTH, None, None),
            P(BOTH, None, None),
            P("center", None),
        ),
        out_specs=(P(BOTH, None), P(BOTH)),
        check_vma=False,
    )
```

```python
import functools

import jax
import jax.numpy as jnp
from jax import lax
from jax.experimental import pallas as pl
from jax.experimental.pallas import tpu as pltpu
from jax.sharding import PartitionSpec as P

DOC_DEV = 8
BOTH = ("center", "expert")
CORE, ALONG_X, ALONG_Y = 1, 2, 4
LANES = 128


def rms_normed(hidden_rows):
    values = hidden_rows.astype(jnp.float32)
    inverse_rms = lax.rsqrt(jnp.mean(values * values, axis=-1, keepdims=True) + 1e-06)
    return (values * inverse_rms).astype(jnp.bfloat16)


KERNEL = pltpu.CompilerParams(vmem_limit_bytes=24 * 1024 * 1024)
ANYWHERE = pl.BlockSpec(memory_space=pltpu.HBM)
IN_VMEM = pl.BlockSpec(memory_space=pltpu.VMEM)
BESIDE = pl.CostEstimate(flops=1000, bytes_accessed=1000, transcendentals=0)
IN_SMEM = pl.BlockSpec(memory_space=pltpu.SMEM)
BF16 = jnp.bfloat16


def gate_lanes(shape, expert, expert_count):
    lane = lax.broadcasted_iota(jnp.int32, shape, len(shape) - 1)
    return (
        (lane == expert) | (lane == expert + expert_count) | (lane == expert + 2 * expert_count)
    )


def pick_kernel(capacity, expert_count, who_ref, *refs):
    count = len(refs) - 3
    blocks = refs[:count]
    mine, other, choice = refs[count:]
    tok_count = blocks[0].shape[0]
    model_width = blocks[0].shape[1] - LANES
    row = lax.broadcasted_iota(jnp.int32, (8, LANES), 0)
    asked = jnp.where(
        row == 0,
        gate_lanes((8, LANES), who_ref[0], expert_count).astype(jnp.float32),
        gate_lanes((8, LANES), who_ref[1], expert_count).astype(jnp.float32),
    ).astype(BF16)
    before = (
        lax.broadcasted_iota(jnp.int32, (tok_count, tok_count), 0)
        < lax.broadcasted_iota(jnp.int32, (tok_count, tok_count), 1)
    ).astype(jnp.float32).astype(BF16)
    slot_row = lax.broadcasted_iota(jnp.int32, (2 * capacity, tok_count), 0)
    first_half = slot_row < capacity
    slot_row = slot_row.astype(jnp.float32)
    tails = jnp.concatenate([block[:, pl.ds(model_width, LANES)] for block in blocks], axis=0)
    gates = lax.dot_general(
        asked, tails, (((1,), (1,)), ((), ())), preferred_element_type=jnp.float32
    )
    named = gates != 0.0
    ones = named.astype(jnp.float32).astype(BF16)
    for j in range(count):
        at = j * tok_count
        slot = jnp.dot(ones[:, at : at + tok_count], before, preferred_element_type=jnp.float32)
        slot = jnp.where(named[:, at : at + tok_count], slot, -1.0 - 2.0 * capacity)
        slot = jnp.where(first_half, slot[0:1, :], slot[1:2, :] + float(capacity))
        choice[j] = (slot == slot_row).astype(jnp.float32).astype(BF16)
    for j in range(count):
        picked = jnp.dot(choice[j], blocks[j][...], preferred_element_type=jnp.float32).astype(BF16)
        here = pl.ds(j * capacity, capacity)
        mine[here, :] = picked[:capacity]
        other[here, :] = picked[capacity:]


def pick(capacity, expert_count, who, blocks):
    count, tok_count, row_width = len(blocks), *blocks[0].shape
    picked = (count * capacity, row_width)
    choice = (count, 2 * capacity, tok_count)
    return pl.pallas_call(
        functools.partial(pick_kernel, capacity, expert_count),
        out_shape=[jax.ShapeDtypeStruct(shape, BF16) for shape in (picked, picked, choice)],
        in_specs=[IN_SMEM] + [IN_VMEM] * count,
        out_specs=[IN_VMEM] * 3,
        compiler_params=KERNEL,
        cost_estimate=BESIDE,
        name="pick",
    )(who, *blocks)


def expert_kernel(expert_count, count, who_ref, *refs):
    parts = refs[:count]
    gate_up, down = refs[count : count + 2]
    outs = refs[count + 2 : 2 * count + 2]
    hidden = refs[2 * count + 2]
    row_count = hidden.shape[0]
    hidden_width, model_width = down.shape
    tile = 256
    hidden_tiles, model_tiles = hidden_width // tile, model_width // tile
    starts = [0]
    for part in parts:
        starts.append(starts[-1] + part.shape[0])

    def columns(at, size):
        return jnp.concatenate([part[:, pl.ds(at, size)] for part in parts], axis=0)

    tail = columns(model_width, LANES).astype(jnp.float32)
    gate_column = jnp.sum(
        jnp.where(gate_lanes((row_count, LANES), who_ref[0], expert_count), tail, 0.0),
        axis=1,
        keepdims=True,
    )
    for step in range(hidden_tiles):
        at = step * tile
        values = columns(0, model_width)
        gate = jnp.dot(values, gate_up[:, pl.ds(at, tile)], preferred_element_type=jnp.float32)
        up = jnp.dot(
            values,
            gate_up[:, pl.ds(at + hidden_width, tile)],
            preferred_element_type=jnp.float32,
        )
        hidden[:, pl.ds(at, tile)] = (gate / (1.0 + jnp.exp(-gate)) * up).astype(BF16)
    for step in range(model_tiles):
        at = step * tile
        product = jnp.dot(
            hidden[...], down[:, pl.ds(at, tile)], preferred_element_type=jnp.float32
        )
        product = (product * gate_column).astype(BF16)
        for i, out in enumerate(outs):
            out[:, pl.ds(at, tile)] = product[starts[i] : starts[i + 1]]


def expert_rows(expert_count, who, parts, weights_gu, weights_down):
    hidden_width, model_width = weights_down.shape
    rows = sum(part.shape[0] for part in parts)
    outs = [jax.ShapeDtypeStruct((part.shape[0], model_width), BF16) for part in parts]
    return pl.pallas_call(
        functools.partial(expert_kernel, expert_count, len(parts)),
        out_shape=outs,
        in_specs=[IN_SMEM] + [IN_VMEM] * (len(parts) + 2),
        out_specs=[IN_VMEM] * len(parts),
        scratch_shapes=[pltpu.VMEM((rows, hidden_width), BF16)],
        compiler_params=KERNEL,
        cost_estimate=BESIDE,
        name="expert_rows",
    )(who, *parts, weights_gu, weights_down)


def put_kernel(choice, mine, other, *outs):
    capacity = choice.shape[1] // 2
    for j, out in enumerate(outs):
        here = pl.ds(j * capacity, capacity)
        rows = jnp.concatenate([mine[here, :], other[here, :]], axis=0)
        out[...] = lax.dot_general(
            choice[j], rows, (((0,), (0,)), ((), ())), preferred_element_type=jnp.float32
        ).astype(BF16)


def put(choice, mine, other):
    count, _, tok_count = choice.shape
    model_width = mine.shape[1]
    return pl.pallas_call(
        put_kernel,
        out_shape=[jax.ShapeDtypeStruct((tok_count, model_width), BF16)] * count,
        in_specs=[IN_VMEM] * 3,
        out_specs=[IN_VMEM] * count,
        compiler_params=KERNEL,
        cost_estimate=BESIDE,
        name="put",
    )(choice, mine, other)


def normed_sum(summed):
    return (summed * lax.rsqrt(jnp.sum(summed * summed, axis=1, keepdims=True) + 1e-06)).astype(
        jnp.bfloat16
    )


def added(*terms):
    total = terms[0].astype(jnp.float32)
    for term in terms[1:]:
        total = total + term.astype(jnp.float32)
    return total


def enter_kernel(expert_count, *refs):
    sources, rows_ref, targets, sem = refs[:4], refs[4], refs[5:9], refs[9]
    copies = [
        pltpu.make_async_copy(source, target, sem.at[i])
        for i, (source, target) in enumerate(zip(sources, targets))
    ]
    for copy in copies:
        copy.start()
    tokens_ref, ids_ref, gates_ref, docs_ref = targets
    tok_count, model_width = tokens_ref.shape
    for copy in copies[1:]:
        copy.wait()
    raw = gates_ref[...]
    gates = raw / jnp.sum(raw, axis=0, keepdims=True)
    ids = ids_ref[...]
    lane = lax.broadcasted_iota(jnp.int32, (LANES, tok_count), 0)
    table = jnp.zeros((LANES, tok_count), jnp.float32)
    for term in range(3):
        for choice in range(ids.shape[0]):
            hit = lane == ids[choice : choice + 1, :] + term * expert_count
            table = jnp.where(hit, gates[choice : choice + 1, :], table)
    first = table.astype(BF16).astype(jnp.float32)
    rest = table - first
    second = rest.astype(BF16).astype(jnp.float32)
    table = jnp.where(
        lane < expert_count, first, jnp.where(lane < 2 * expert_count, second, rest - second)
    )
    table = jnp.where(lane == 3 * expert_count, docs_ref[...].astype(jnp.float32), table)
    rows_ref[:, pl.ds(model_width, LANES)] = jnp.transpose(table).astype(BF16)
    copies[0].wait()
    rows_ref[:, pl.ds(0, model_width)] = rms_normed(tokens_ref[...])


def enter(tokens, expert_ids, gate_raw, doc_ids, expert_count):
    tok_count, model_width = tokens.shape
    return pl.pallas_call(
        functools.partial(enter_kernel, expert_count),
        out_shape=jax.ShapeDtypeStruct((tok_count, model_width + LANES), BF16),
        in_specs=[ANYWHERE] * 4,
        out_specs=IN_VMEM,
        scratch_shapes=[
            pltpu.VMEM(operand.shape, operand.dtype)
            for operand in (tokens, expert_ids.T, gate_raw.T, doc_ids)
        ]
        + [pltpu.SemaphoreType.DMA((4,))],
        compiler_params=pltpu.CompilerParams(vmem_limit_bytes=62 * 1024 * 1024),
        cost_estimate=BESIDE,
        name="enter",
    )(tokens, expert_ids.T, gate_raw.T, doc_ids)


def leave_kernel(doc_lane, sizes, *refs):
    refs = list(refs)
    groups, tails = [], []
    for size in sizes:
        groups.append([refs.pop(0) for _ in range(size)])
        tails.append(refs.pop(0))
    blocks, sums = refs[: len(sizes) - 1], refs[len(sizes) - 1 :]
    for i, group in enumerate(groups):
        total = group[0][...]
        if len(group) > 1:
            total = added(*[term[...] for term in group]).astype(BF16)
            blocks[i - 1][...] = total
        lane = lax.broadcasted_iota(jnp.int32, tails[i].shape, 1)
        named = tails[i][...].astype(jnp.float32)
        named = jnp.sum(jnp.where(lane == doc_lane, named, 0.0), axis=1, keepdims=True)
        member = (named == lane.astype(jnp.float32)).astype(jnp.float32).astype(BF16)
        sums[i][...] = lax.dot_general(
            member, total, (((0,), (0,)), ((), ())), preferred_element_type=jnp.float32
        )[:DOC_DEV]


def leave(doc_lane, groups):
    tok_count, model_width = groups[0][0][0].shape
    operands = [ref for blocks, tail in groups for ref in (*blocks, tail)]
    count = len(groups)
    results = pl.pallas_call(
        functools.partial(leave_kernel, doc_lane, [len(blocks) for blocks, _ in groups]),
        out_shape=[jax.ShapeDtypeStruct((tok_count, model_width), BF16)] * (count - 1)
        + [jax.ShapeDtypeStruct((DOC_DEV, model_width), jnp.float32)] * count,
        in_specs=[IN_VMEM] * len(operands),
        out_specs=[IN_VMEM] * (2 * count - 1),
        compiler_params=KERNEL,
        cost_estimate=BESIDE,
        name="leave",
    )(*operands)
    return results[: count - 1], results[count - 1 :]


SWAP_X = ("center", tuple((i, i ^ ALONG_X) for i in range(8)))
SWAP_Y = ("center", tuple((i, i ^ ALONG_Y) for i in range(8)))
SWAP_XY = ("center", tuple((i, i ^ ALONG_X ^ ALONG_Y) for i in range(8)))
SWAP_CORE = ("center", tuple((i, i ^ CORE) for i in range(8)))
SWAP_Z = ("expert", ((0, 1), (1, 0), (2, 3), (3, 2)))
MIDDLE = ("expert", ((1, 2), (2, 1)))


def at_once(*sends, behind=()):
    values = [value for _, value in sends]
    if len(behind) > 0:
        held = lax.optimization_barrier((tuple(values), tuple(behind)))
        values = held[0]
    return [lax.ppermute(value, way[0], way[1]) for (way, _), value in zip(sends, values)]


def gathered_layer(rows, who, weights_gu, weights_down, capacity, expert_count, beside):
    def picked(*blocks):
        return pick(capacity, expert_count, who, blocks)

    def crossed(values):
        return at_once((SWAP_CORE, values))[0]

    def results(*parts):
        return expert_rows(expert_count, who, parts, weights_gu, weights_down)

    def worked(*groups):
        parts = [part for mine, other, _ in groups for part in (mine, other)]
        done = results(*parts)
        return [(groups[i][2], done[2 * i], done[2 * i + 1]) for i in range(len(groups))]

    b0 = rows
    bx0, by0, b1, c2 = at_once((SWAP_X, b0), (SWAP_Y, b0), (SWAP_Z, b0), (MIDDLE, b0))
    d0, by1, o2, c3 = at_once(
        (SWAP_X, by0), (SWAP_Y, b1), (SWAP_Z, c2), (MIDDLE, b1),
        behind=(bx0, by0, b1, c2),
    )
    mine, other, choice = picked(b0, bx0, by0, b1)
    first = (mine, crossed(other), choice)
    b2 = c2 + o2
    bx2, by2, o3 = at_once(
        (SWAP_X, b2), (SWAP_Y, b2), (SWAP_Z, c3), behind=(d0, by1, c3, mine, beside)
    )
    mine, other, choice = picked(d0, by1, b2)
    second = (mine, crossed(other), choice)
    b3 = c3 + o3
    bx3, by3, bx1 = at_once(
        (SWAP_X, b3), (SWAP_Y, b3), (SWAP_Z, bx0), behind=(bx2, by2, mine)
    )
    mine, other, choice = picked(bx2, by2, b3)
    third = (mine, crossed(other), choice)
    (first,) = worked(first)
    (d1,) = at_once((SWAP_Z, d0), behind=(bx1, mine))
    d2, d3 = at_once((SWAP_X, by2), (SWAP_Y, bx3), behind=(bx3, by3, bx1, mine, first[1]))
    mine, other, choice = picked(bx3, by3, bx1)
    fourth = (mine, crossed(other), choice)
    (third,) = worked(third)
    (fourth_mine,) = results(lax.optimization_barrier((fourth[0], third[1]))[0])
    held = lax.optimization_barrier((d1, d2, d3, mine, third[1], fourth_mine))
    mine, other, choice = picked(*held[:3])
    last_mine, last_other = results(mine)[0], crossed(other)
    (last_other,) = results(lax.optimization_barrier((last_other, last_mine))[0])
    (fourth_other,) = results(lax.optimization_barrier((fourth[1], last_other))[0])
    g5 = put(choice, last_mine, crossed(last_other))
    rx_y2, ry_x3, rz_d0 = at_once((SWAP_X, g5[1]), (SWAP_Y, g5[2]), (SWAP_Z, g5[0]))
    fourth_other = crossed(fourth_other)
    g3 = put(*lax.optimization_barrier((third[0], third[1], crossed(third[2]), g5[0]))[:3])
    g4 = put(*lax.optimization_barrier((fourth[2], fourth_mine, fourth_other, g5[0]))[:3])
    second = (lax.optimization_barrier((second[0], g5[0]))[0], *second[1:])
    (second,) = worked(second)
    g2 = put(second[0], second[1], crossed(second[2]))
    g1 = put(*lax.optimization_barrier((first[0], first[1], crossed(first[2]), g4[0]))[:3])
    sx3 = added(g4[0], ry_x3).astype(BF16)
    rx_b3, ry_b3, rz_x0 = at_once(
        (SWAP_X, sx3), (SWAP_Y, g4[1]), (SWAP_Z, g4[2]), behind=(rx_y2, rz_d0, g4[0], second[1], g1[0], g3[0])
    )
    sy2 = added(g3[1], rx_y2).astype(BF16)
    s3 = added(g3[2], rx_b3, ry_b3).astype(BF16)
    rx_b2, ry_b2, in_3 = at_once(
        (SWAP_X, g3[0]), (SWAP_Y, sy2), (SWAP_Z, s3), behind=(rz_x0, g2[0])
    )
    (sx0,), (_, sum_x) = leave(
        3 * expert_count,
        [([g1[0]], rows[:, -LANES:]), ([g1[1], rz_x0], bx0[:, -LANES:])],
    )
    (sum_x,) = at_once((SWAP_X, sum_x), behind=(rx_b2,))
    sd0 = added(g2[0], rz_d0).astype(BF16)
    s2 = added(g2[2], rx_b2, ry_b2).astype(BF16)
    rx_y0, ry_b1, in_2, over_3 = at_once(
        (SWAP_X, sd0), (SWAP_Y, g2[1]), (SWAP_Z, s2),
        (MIDDLE, added(s3, in_3).astype(BF16)), behind=(rx_b2, ry_b2),
    )
    (sy0, s1, m2), (sum_own, *sums) = leave(
        3 * expert_count,
        [
            ([g1[0]], rows[:, -LANES:]),
            ([g1[2], rx_y0], by0[:, -LANES:]),
            ([g1[3], ry_b1, over_3], b1[:, -LANES:]),
            ([s2, in_2], c2[:, -LANES:]),
        ],
    )
    sums = at_once((SWAP_Y, sums[0]), (SWAP_Z, sums[1]), (MIDDLE, sums[2]))
    pooled = normed_sum(added(sum_own, sum_x, *sums))
    held = lax.optimization_barrier((sx0, rx_y0))[0]
    rx_b0, ry_b0, rz_b0, over_2 = at_once(
        (SWAP_X, held), (SWAP_Y, sy0), (SWAP_Z, s1), (MIDDLE, m2)
    )
    return added(g1[0], rx_b0, ry_b0, rz_b0, over_2), pooled


def slot_table(chosen_ids, expert_count):
    chosen = (
        chosen_ids[:, :, None] == jnp.arange(expert_count, dtype=jnp.int32)[None, None, :]
    ).astype(jnp.int32)
    per_token = jnp.sum(chosen, axis=1)
    before = jnp.cumsum(per_token, axis=0) - per_token
    return jnp.sum(chosen * before[:, None, :], axis=2)


def expert_ffn(rows_in, weights_gu, weights_down):
    model_width = rows_in.shape[-1]
    flat_rows = rows_in.reshape(-1, model_width)
    hidden_width = weights_down.shape[0]
    gate_and_up = jnp.dot(flat_rows, weights_gu, preferred_element_type=jnp.float32)
    hidden = (jax.nn.silu(gate_and_up[:, :hidden_width]) * gate_and_up[:, hidden_width:]).astype(
        jnp.bfloat16
    )
    result = jnp.dot(hidden, weights_down, preferred_element_type=jnp.float32).astype(jnp.bfloat16)
    return result.reshape(rows_in.shape)


def exchanged_layer(normed, expert_ids, gate_norm, weights_gu, weights_down, capacity):
    tok_count, top_count = expert_ids.shape
    model_width = normed.shape[1]
    expert_count = lax.axis_size("center") * lax.axis_size("expert")
    position = slot_table(expert_ids, expert_count)
    target = (expert_ids * capacity + position).reshape(-1)
    repeated = jnp.broadcast_to(normed[:, None, :], (tok_count, top_count, model_width)).reshape(
        -1, model_width
    )
    send_buffer = (
        jnp.zeros((expert_count * capacity, model_width), jnp.bfloat16).at[target].set(repeated)
    )
    send_buffer = send_buffer.reshape(expert_count, capacity, model_width)
    computed = expert_ffn(
        lax.all_to_all(send_buffer, BOTH, split_axis=0, concat_axis=0, tiled=True),
        weights_gu,
        weights_down,
    )
    returned = lax.all_to_all(computed, BOTH, split_axis=0, concat_axis=0, tiled=True)
    returned = returned.reshape(expert_count * capacity, model_width)
    gathered = returned[target].reshape(tok_count, top_count, model_width)
    return jnp.sum(gathered.astype(jnp.float32) * gate_norm[:, :, None], axis=1)


def local(tokens, doc_ids, expert_ids, gate_raw, gate_up, down, bank):
    center_count = lax.axis_size("center")
    expert_axis = lax.axis_size("expert")
    expert_count = center_count * expert_axis
    tok_count, top_count = expert_ids.shape
    capacity = min(tok_count, 2 * tok_count * top_count // expert_count)
    weights_gu = gate_up[0]
    weights_down = down[0]
    bank_values = bank.astype(jnp.float32)
    bank_norms = jnp.sum(bank_values * bank_values, axis=1)
    if center_count == 8 and expert_axis == 4:
        rows = enter(tokens, expert_ids, gate_raw, doc_ids, expert_count)
        center_at, expert_at = lax.axis_index("center"), lax.axis_index("expert")
        who = jnp.stack(
            [center_at * expert_axis + expert_at, (center_at ^ CORE) * expert_axis + expert_at]
        ).astype(jnp.int32)
        combined, pooled = gathered_layer(
            rows, who, weights_gu, weights_down, capacity, expert_count, bank_norms
        )
    else:
        gate_norm = gate_raw / jnp.sum(gate_raw, axis=1, keepdims=True)
        combined = exchanged_layer(
            rms_normed(tokens), expert_ids, gate_norm, weights_gu, weights_down, capacity
        )
        member = (jnp.arange(DOC_DEV, dtype=jnp.int32)[:, None] == doc_ids[0][None, :]).astype(
            jnp.float32
        )
        summed = jnp.dot(
            member, combined, precision=lax.Precision.HIGHEST, preferred_element_type=jnp.float32
        )
        pooled = normed_sum(summed)
    layer_out = combined.astype(jnp.bfloat16)
    shard_part = lax.all_gather(pooled, "center", axis=0, tiled=True)
    doc_values = shard_part.astype(jnp.float32)
    doc_norms = jnp.sum(doc_values * doc_values, axis=1)
    products = lax.dot_general(
        shard_part, bank, (((1,), (1,)), ((), ())), preferred_element_type=jnp.float32
    )
    distance = doc_norms[:, None] + bank_norms[None, :] - 2.0 * products
    nearest = jnp.min(distance, axis=1)
    if center_count == 8 and expert_axis == 4:
        ways = (SWAP_X, SWAP_Y, SWAP_XY)
        for arrived in at_once(*[(way, nearest) for way in ways], behind=(layer_out,)):
            nearest = jnp.minimum(nearest, arrived)
        nearest = jnp.minimum(nearest, at_once((SWAP_CORE, nearest))[0])
    else:
        nearest = lax.pmin(nearest, "center")
    own_scores = lax.dynamic_slice_in_dim(nearest, lax.axis_index("center") * DOC_DEV, DOC_DEV)
    return (layer_out, own_scores)


def solution(mesh):
    return jax.shard_map(
        local,
        mesh=mesh,
        in_specs=(
            P(BOTH, None),
            P(BOTH, None),
            P(BOTH, None),
            P(BOTH, None),
            P(BOTH, None, None),
            P(BOTH, None, None),
            P("center", None),
        ),
        out_specs=(P(BOTH, None), P(BOTH)),
        check_vma=False,
    )
```
